32 devices in a mesh: grp: 2 (over y), day: 4 (over z), cell: 4 (over x, core).
Axes of the slice: x: 2, y: 2, z: 4, core: 2. Of those that a mesh axis runs over, the one named last changes fastest.
Arguments:
- series: bfloat16 [6144, 8192], P(('grp', 'day'), 'cell'), parts along dimension 0, may hold values from -6 to 6
- eofs: bfloat16 [64, 64, 8192], P(None, 'day', 'cell'), may hold values from -0.1875 to 0.1875
Outputs:
- pcs: float32 [6144, 64], P(('grp', 'day')), parts along dimension 0
- reconstruction: float32 [6144, 8192], P(('grp', 'day'), 'cell'), parts along dimension 0
The draws below stay inside these ranges and needn't reach their ends.
There are 2 independent parts, one for each index of `grp`. The reference program is written for one: setup_inputs(seed, part) draws one part's arguments, and reference() takes and returns one part's arrays. A program takes and returns all parts, laid end to end along the dimension named above; an argument that names none is the same for every part. Nothing has to cross between parts.
All inputs are finite; a program needn't handle non-finite values.
Results may differ from the reference program's by a relative error of at most 0.0029.
Values may be sent and summed in bfloat16 or wider, within the bound.
No kernel may reach another device: no remote copies, remote signals or barrier semaphores. Data moves between devices by JAX's collectives and lax.ppermute only.
A program may use at most 128 MiB of HBM per device.

```python
import jax
import jax.numpy as jnp

CELLS = 8192
LAG = 64
MODES = 64
TOTAL_DAYS = 3072


def shard_levels(own_key, dims, shards, smallest, largest):
    level = 1.0
    for dim, shards_of in shards:
        steps = jax.random.uniform(jax.random.fold_in(jax.random.fold_in(own_key, 6), dim), (shards_of,), jnp.float32, smallest / len(shards), largest / len(shards))
        level = level * jnp.repeat(jnp.exp(steps), dims[dim] // shards_of).reshape((-1,) + (1,) * (len(dims) - 1 - dim))
    return level


def bell_draw(stream_key, dims, width, most, pieces=(), held_as=jnp.bfloat16):
    values = jax.random.normal(stream_key, dims, jnp.float32) * width
    if len(pieces) > 0:
        values = shard_levels(stream_key, dims, pieces, -0.22, 0.18) * values
    return jnp.clip(values, min=-most, max=most).astype(held_as)


def setup_inputs(seed: int = 0, part: int = 0) -> dict:
    keys = jax.random.split(jax.random.key(seed), 3)
    part_splits = jax.random.split(jax.random.fold_in(keys[2], part), 3)
    series = bell_draw(part_splits[0], (TOTAL_DAYS, CELLS), 1.0, 6.0, ((0, 4), (1, 4)))
    eofs = bell_draw(keys[1], (LAG, MODES, CELLS), (LAG * MODES // 4) ** -0.5, 0.1875, ((1, 4), (2, 4)))
    return dict(series=series, eofs=eofs)


def reference(series, eofs):
    total = series.shape[0]
    windows = total - LAG + 1
    pcs = jnp.zeros((windows, MODES), jnp.float32)
    for lag_step in range(LAG):
        pcs = pcs + jnp.dot(series[lag_step:lag_step + windows], eofs[lag_step].T, preferred_element_type=jnp.float32)
    pcs_full = jnp.concatenate([pcs, jnp.zeros((LAG - 1, MODES), jnp.float32)], axis=0)
    narrow = pcs_full.astype(jnp.bfloat16)
    padded = jnp.concatenate([jnp.zeros((LAG - 1, MODES), jnp.bfloat16), narrow], axis=0)
    rebuilt = jnp.zeros((total, CELLS), jnp.float32)
    for lag_step in range(LAG):
        begin = LAG - 1 - lag_step
        rebuilt = rebuilt + jnp.dot(padded[begin:begin + total], eofs[lag_step], preferred_element_type=jnp.float32)
    days = jnp.arange(total, dtype=jnp.int32)
    count = (jnp.minimum(days, total - LAG) - jnp.maximum(0, days - LAG + 1) + 1).astype(jnp.float32)
    return pcs_full, rebuilt / count[:, None]
```

```python
import functools

import jax
import jax.numpy as jnp
from jax import lax
from jax.experimental import pallas as pl
from jax.experimental.pallas import tpu as pltpu
from jax.sharding import PartitionSpec as P

LANES = 128
WIDE = 256
HALO = 64
VMEM_BYTES = 40 * 1024 * 1024

ENDS, MIDS = (0, 3), (1, 2)
PAIRED = ((0, 1), (1, 0), (2, 3), (3, 2))
MIDDLE = ((1, 2), (2, 1))
OUTWARD = ((1, 0), (2, 3))


def lane_group(shape, modes):
    return lax.broadcasted_iota(jnp.int32, shape, len(shape) - 1) // modes


def add_lane_groups(x, modes):
    shift = LANES // 2
    while shift >= modes:
        x = x + pltpu.roll(x, shift, 1)
        shift //= 2
    return x


def pack_rows(x, modes):
    rows, groups = x.shape[0], LANES // modes
    x = x.reshape(rows // groups, groups, LANES)
    place = lax.broadcasted_iota(jnp.int32, x.shape, 1)
    return jnp.sum(jnp.where(place == lane_group(x.shape, modes), x, 0.0), axis=1)


def unpack_rows(x, modes):
    rows, groups = x.shape[0], LANES // modes
    x = jnp.broadcast_to(x[:, None, :], (rows, groups, LANES))
    place = lax.broadcasted_iota(jnp.int32, x.shape, 1)
    x = jnp.where(place == lane_group(x.shape, modes), x, 0.0)
    return add_lane_groups(x.reshape(rows * groups, LANES), modes)


def load_pieces(plan, refs, bank, sems, meta):
    waits = []
    for i, (row, rows, sources) in enumerate(plan):
        target = bank.at[pl.ds(row, rows), :]
        if len(sources) == 1:
            pltpu.make_async_copy(refs[sources[0]], target, sems.at[i]).start()
        else:
            for choice, source in enumerate(sources):

                @pl.when(meta[3] == choice)
                def _():
                    pltpu.make_async_copy(refs[source], target, sems.at[i]).start()

        waits.append(pltpu.make_async_copy(refs[sources[0]], target, sems.at[i]))
    return waits


def lag_start(part, meta, half, lags):
    if half is None:
        return part * lags
    here, index = half
    side = meta[2] if here else 1 - meta[2]
    return pl.multiple_of((side * half_parts(part) + index) * lags, 16)


def half_parts(total):
    return total // 2


def project_kernel(plan, parts, total_parts, modes, n_refs, finish, has_acc, *refs):
    meta, behind, series, ahead = refs[:4]
    pieces = refs[4 : 4 + n_refs]
    at = 4 + n_refs
    acc_in = None
    if has_acc:
        acc_in = refs[at]
        at += 1
    out, source, bank, acc, sems, src_sems = refs[at:]
    lags = WIDE // modes
    days = series.shape[0]
    halo = behind.shape[0]
    copies = [
        pltpu.make_async_copy(behind, source.at[pl.ds(0, halo), :], src_sems.at[0]),
        pltpu.make_async_copy(series, source.at[pl.ds(halo, days), :], src_sems.at[1]),
        pltpu.make_async_copy(ahead, source.at[pl.ds(halo + days, halo), :], src_sems.at[2]),
    ]
    for copy in copies:
        copy.start()
    waits = load_pieces(plan, pieces, bank, sems, meta)
    for copy in copies + waits:
        copy.wait()
    rows = acc.shape[0]
    for slot, half in enumerate(parts):
        start = lag_start(slot if half is None else total_parts, meta, half, lags)
        term = lax.dot_general(
            source[pl.ds(start, rows), :],
            bank[slot * WIDE : (slot + 1) * WIDE, :],
            (((1,), (1,)), ((), ())),
            preferred_element_type=jnp.float32,
        )
        if slot == 0:
            acc[...] = acc_in[...] + term if has_acc else term
        else:
            acc[...] += term
    if not finish:
        out[...] = acc[...]
        return
    total = acc[...]
    group = lane_group(total.shape, modes)
    bit = 1
    while bit < lags:
        total = jnp.where((group & bit) != 0, pltpu.roll(total, rows - bit, 0), total)
        bit *= 2
    total = total[: days + halo]
    total = total[:, :LANES] + total[:, LANES:]
    out[...] = pack_rows(add_lane_groups(total, modes), modes)


def rebuild_kernel(
    plan, parts, total_parts, modes, n_sums, n_refs, has_in, last, total_days, width, *refs
):
    meta = refs[0]
    sums = refs[1 : 1 + n_sums]
    pieces = refs[1 + n_sums : 1 + n_sums + n_refs]
    at = 1 + n_sums + n_refs
    rec_in = pcs_in = None
    if has_in:
        rec_in, pcs_in = refs[at : at + 2]
        at += 2
    rec_out, pcs_out, bank, stacked, sems = refs[at:]
    lags = WIDE // modes
    days = rec_out.shape[0]
    step = pl.program_id(0)

    @pl.when(step == 0)
    def _():
        waits = load_pieces(plan, pieces, bank, sems, meta)
        level = [ref[...] for ref in sums]
        while len(level) > 1:
            level = [level[i] + level[i + 1] for i in range(0, len(level), 2)]
        value = unpack_rows(level[0], modes)
        rows = value.shape[0]
        day = meta[0] + lax.broadcasted_iota(jnp.int32, value.shape, 0) - HALO
        value = jnp.where((day >= 0) & (day <= total_days - width), value, 0.0)
        own = value[HALO:, : pcs_out.shape[1]]
        mine = lane_group(own.shape, modes) == meta[1]
        pcs_out[...] = jnp.where(mine, own, pcs_in[...] if has_in else 0.0)
        narrow = value.astype(jnp.bfloat16).astype(jnp.float32)
        spread = jnp.concatenate([narrow, narrow], axis=1)
        group = lane_group(spread.shape, modes)
        bit = 1
        while bit < lags:
            spread = jnp.where((group & bit) != 0, pltpu.roll(spread, bit, 0), spread)
            bit *= 2
        stacked[...] = spread[lags:].astype(jnp.bfloat16)
        for copy in waits:
            copy.wait()

    columns = pl.ds(pl.multiple_of(step * rec_out.shape[1], rec_out.shape[1]), rec_out.shape[1])
    acc = None
    for slot, half in enumerate(parts):
        start = lag_start(slot if half is None else total_parts, meta, half, lags)
        offset = pl.multiple_of(width - lags - start, 16)
        term = jnp.dot(
            stacked[pl.ds(offset, days), :],
            bank[slot * WIDE : (slot + 1) * WIDE, columns],
            preferred_element_type=jnp.float32,
        )
        acc = term if acc is None else acc + term
    if has_in:
        acc = acc + rec_in[...]
    if last:
        day = meta[0] + lax.broadcasted_iota(jnp.int32, (days, 1), 0)
        count = jnp.minimum(day, total_days - width) - jnp.maximum(0, day - width + 1) + 1
        acc = acc * (1.0 / count.astype(jnp.float32))
    rec_out[...] = acc


def smem():
    return pl.BlockSpec(memory_space=pltpu.SMEM)


def anywhere():
    return pl.BlockSpec(memory_space=pl.ANY)


def in_vmem():
    return pl.BlockSpec(memory_space=pltpu.VMEM)


def flatten(pieces):
    arrays, plan, row = [], [], 0
    for choices in pieces:
        ids = []
        for array in choices:
            ids.append(len(arrays))
            arrays.append(array)
        rows = choices[0].shape[0]
        plan.append((row, rows, tuple(ids)))
        row += rows
    return plan, arrays, row


def project(meta, source, pieces, parts, modes, width, acc=None, finish=True):
    behind, series, ahead = source
    days, cells = series.shape
    lags = WIDE // modes
    plan, arrays, bank_rows = flatten(pieces)
    rows = days + HALO + lags
    if finish:
        shape = ((days + HALO) * modes // LANES, LANES)
    else:
        shape = (rows, WIDE)
    return pl.pallas_call(
        functools.partial(
            project_kernel,
            plan,
            parts,
            width // lags,
            modes,
            len(arrays),
            finish,
            acc is not None,
        ),
        out_shape=jax.ShapeDtypeStruct(shape, jnp.float32),
        in_specs=[smem()]
        + [anywhere()] * (3 + len(arrays))
        + ([in_vmem()] if acc is not None else []),
        out_specs=in_vmem(),
        scratch_shapes=[
            pltpu.VMEM((days + 2 * HALO, cells), jnp.bfloat16),
            pltpu.VMEM((bank_rows, cells), jnp.bfloat16),
            pltpu.VMEM((rows, WIDE), jnp.float32),
            pltpu.SemaphoreType.DMA((len(plan),)),
            pltpu.SemaphoreType.DMA((3,)),
        ],
        compiler_params=pltpu.CompilerParams(vmem_limit_bytes=VMEM_BYTES),
        cost_estimate=pl.CostEstimate(
            flops=2 * rows * bank_rows * cells,
            bytes_accessed=2 * cells * (bank_rows + days + 2 * HALO),
            transcendentals=0,
        ),
        name="project",
    )(meta, behind, series, ahead, *arrays, *([] if acc is None else [acc]))


def rebuild(meta, sums, pieces, parts, modes, width, days, cells, total_days, all_modes, so_far, last):
    lags = WIDE // modes
    plan, arrays, bank_rows = flatten(pieces)
    tile = min(WIDE, cells)
    rec_spec = pl.BlockSpec((days, tile), lambda i: (0, i))
    pcs_spec = pl.BlockSpec((days, all_modes), lambda i: (0, 0))
    has_in = so_far is not None
    n_before = 1 + len(sums) + len(arrays)
    return pl.pallas_call(
        functools.partial(
            rebuild_kernel,
            plan,
            parts,
            width // lags,
            modes,
            len(sums),
            len(arrays),
            has_in,
            last,
            total_days,
            width,
        ),
        grid=(cells // tile,),
        out_shape=(
            jax.ShapeDtypeStruct((days, cells), jnp.float32),
            jax.ShapeDtypeStruct((days, all_modes), jnp.float32),
        ),
        in_specs=[smem()]
        + [in_vmem()] * len(sums)
        + [anywhere()] * len(arrays)
        + ([rec_spec, pcs_spec] if has_in else []),
        out_specs=(rec_spec, pcs_spec),
        scratch_shapes=[
            pltpu.VMEM((bank_rows, cells), jnp.bfloat16),
            pltpu.VMEM((days + HALO - lags, WIDE), jnp.bfloat16),
            pltpu.SemaphoreType.DMA((len(plan),)),
        ],
        input_output_aliases={n_before: 0, n_before + 1: 1} if has_in else {},
        compiler_params=pltpu.CompilerParams(
            vmem_limit_bytes=VMEM_BYTES, dimension_semantics=("arbitrary",)
        ),
        cost_estimate=pl.CostEstimate(
            flops=2 * days * bank_rows * cells,
            bytes_accessed=2 * cells * bank_rows + 8 * days * cells,
            transcendentals=0,
        ),
        name="rebuild",
    )(meta, *sums, *arrays, *(so_far if has_in else ()))


def exchange(packed):
    size = lax.axis_size("cell")
    return [packed] + [
        lax.ppermute(packed, "cell", [(i, i ^ step) for i in range(size)]) for step in range(1, size)
    ]


def on_device(series, eofs):
    width, modes, cells = eofs.shape
    days = series.shape[0]
    n = lax.axis_size("day")
    groups = lax.axis_size("grp")
    total_days = days * n
    all_modes = modes * n
    day = lax.axis_index("day")
    grp = lax.axis_index("grp")
    lags = WIDE // modes
    n_parts = width // lags
    bank = eofs.reshape(width * modes, cells)
    behind = lax.ppermute(series[days - HALO :], "day", [(i, i + 1) for i in range(n - 1)])
    ahead = lax.ppermute(series[:HALO], "day", [(i + 1, i) for i in range(n - 1)])
    middle = ((day > 0) & (day < n - 1)).astype(jnp.int32)

    def meta(block):
        return jnp.stack(
            [(day * days).astype(jnp.int32), jnp.asarray(block, jnp.int32), grp.astype(jnp.int32), middle]
        )

    whole = [None] * n_parts
    shape = dict(modes=modes, width=width)
    rest = dict(days=days, cells=cells, total_days=total_days, all_modes=all_modes)

    if n != 4 or groups != 2 or n_parts != 4:
        every = lax.all_gather(bank, "day", axis=0, tiled=False)
        source = (behind, series, ahead)
        so_far = None
        for block in range(n):
            pieces = [(every[block],)]
            sums = exchange(project(meta(block), source, pieces, whole, **shape))
            so_far = rebuild(
                meta(block), sums, pieces, whole, so_far=so_far, last=block == n - 1, **shape, **rest
            )
        return so_far[1], so_far[0]

    cuts = 4
    half = width * modes // 2
    size = half // cuts
    first = lax.dynamic_slice_in_dim(bank, grp * half, half, axis=0)
    held = {("own", i): first[i * size : (i + 1) * size] for i in range(cuts)}
    held["behind"], held["ahead"] = behind, ahead
    sent_from = {
        "p1": "own", "p2": "own", "q1": "p2", "q2": "p1", "f": "q2",
        "yp1": "p1", "yp2": "p2", "yq1": "q1", "yq2": "q2", "yf": "f",
    }

    def across(array, members):
        return lax.ppermute(
            array,
            ("grp", "day"),
            [(g * n + d, (1 - g) * n + d) for g in (0, 1) for d in members],
        )

    def send(name, array):
        if name == "p1":
            return lax.ppermute(array, "day", PAIRED)
        if name in ("p2", "q2"):
            return lax.ppermute(array, "day", MIDDLE)
        if name in ("q1", "f"):
            return lax.ppermute(array, "day", OUTWARD)
        return across(array, {"yp1": ENDS + MIDS, "yp2": MIDS, "yq1": ENDS, "yq2": MIDS, "yf": ENDS}[name])

    def table(values):
        return jnp.asarray(values, jnp.int32)[day]

    metas = {
        "own": meta(day),
        "a": meta(table([1, 0, 3, 2])),
        "b": meta(table([2, 2, 1, 1])),
        "c": meta(table([3, 3, 0, 0])),
    }
    halves = [(True, 0), (True, 1), (False, 0), (False, 1)]

    def pieces_of(block, which=range(2 * cuts)):
        names = {"a": ("p1",), "b": ("q1", "p2"), "c": ("f", "q2")}[block]
        picked = []
        for i in which:
            prefix = "" if i < cuts else "y"
            picked.append(tuple(held[(prefix + name, i % cuts)] for name in names))
        return picked

    def run(task):
        kind, block = task
        if kind == "project":
            source = (held["behind"], series, held["ahead"])
            if block == "own":
                held["packed", block] = project(metas[block], source, [(bank,)], whole, **shape)
            elif block == "c1":
                held["acc"] = project(
                    metas["c"], source, pieces_of("c", range(6)), halves[:3], finish=False, **shape
                )
            elif block == "c2":
                held["packed", "c"] = project(
                    metas["c"], source, pieces_of("c", range(6, 8)), halves[3:], acc=held["acc"], **shape
                )
            else:
                held["packed", block] = project(metas[block], source, pieces_of(block), halves, **shape)
        elif kind == "exchange":
            for i, array in enumerate(exchange(held["packed", block])):
                held["sum", block, i] = array
        else:
            count = lax.axis_size("cell")
            sums = [held["sum", block, i] for i in range(count)]
            own = block == "own"
            so_far = None if own else (held["rec"], held["pcs"])
            held["rec"], held["pcs"] = rebuild(
                metas[block], sums, [(bank,)] if own else pieces_of(block),
                whole if own else halves, so_far=so_far, last=block == "c", **shape, **rest,
            )

    tasks = {
        2: ("project", "own"), 3: ("exchange", "own"), 5: ("rebuild", "own"),
        7: ("project", "a"), 8: ("exchange", "a"), 10: ("rebuild", "a"),
        11: ("project", "b"), 12: ("exchange", "b"), 14: ("rebuild", "b"),
        13: ("project", "c1"), 15: ("project", "c2"), 16: ("exchange", "c"), 17: ("rebuild", "c"),
    }

    lag = 2
    done_at = []
    for slot in range(18):
        sends = []
        if slot < cuts:
            sends += [("p1", slot), ("p2", slot)]
        elif slot < 2 * cuts:
            sends += [("q1", slot - cuts), ("q2", slot - cuts)]
        elif slot < 3 * cuts:
            sends += [("f", slot - 2 * cuts)]
        late = slot - lag
        if 0 <= late < cuts:
            sends += [("yp1", late)]
        elif cuts <= late < 2 * cuts:
            sends += [("yp2", late - cuts), ("yq1", late - cuts)]
        elif 2 * cuts <= late < 3 * cuts:
            sends += [("yq2", late - 2 * cuts), ("yf", late - 2 * cuts)]
        if lag <= slot < 16:
            keys = [(sent_from[name], i) for name, i in sends] + done_at[slot - lag]
            keys = list(dict.fromkeys(keys))
            values = lax.optimization_barrier(tuple(held[key] for key in keys))
            held.update(zip(keys, values))
        before = dict(held)
        for name, i in sends:
            held[name, i] = send(name, held[sent_from[name], i])
        if slot in tasks:
            run(tasks[slot])
        done_at.append([key for key, value in held.items() if before.get(key) is not value])
    return held["pcs"], held["rec"]


def solution(mesh):
    return jax.shard_map(
        on_device,
        mesh=mesh,
        in_specs=(P(("grp", "day"), "cell"), P(None, "day", "cell")),
        out_specs=(P(("grp", "day"), None), P(("grp", "day"), "cell")),
        check_vma=False,
    )
```

```python
import functools

import jax
import jax.numpy as jnp
from jax import lax
from jax.experimental import pallas as pl
from jax.experimental.pallas import tpu as pltpu
from jax.sharding import PartitionSpec as P

LANES = 128
WIDE = 256
TILE = 512
HALO = 64
VMEM_BYTES = 20 * 1024 * 1024
DAY, GRP, MIDDLE_FLAG, BLOCKS = 0, 1, 2, 3

ENDS, MIDS = (0, 3), (1, 2)
PAIRED = ((0, 1), (1, 0), (2, 3), (3, 2))
MIDDLE = ((1, 2), (2, 1))
OUTWARD = ((1, 0), (2, 3))


def lane_group(shape, modes):
    return lax.broadcasted_iota(jnp.int32, shape, len(shape) - 1) // modes


def pack_skewed(acc, scratch, rows, modes):
    groups = LANES // modes
    long = rows + groups
    scratch[...] = acc[:long, :LANES] + acc[groups : long + groups, LANES:]
    count = long // groups
    group = lane_group((count, LANES), modes)
    here = before = None
    for i in range(groups):
        plane = scratch[pl.ds(i, count, stride=groups), :]
        plane = pltpu.roll(plane, modes * (groups - 1 - i), 1) if i < groups - 1 else plane
        stays = group >= groups - 1 - i
        kept, moved = jnp.where(stays, plane, 0.0), jnp.where(stays, 0.0, plane)
        here = kept if here is None else here + kept
        before = moved if before is None else before + moved
    return here[: rows // groups] + before[1:]


def spread_skewed(packed, scratch, modes):
    groups = LANES // modes
    count = packed.shape[0]
    group = lane_group((count - 1, LANES), modes)
    here, before = packed[1:], packed[:-1]
    for i in range(groups):
        shift = modes * (i + 1) % LANES
        plane = jnp.where(group >= groups - 1 - i, here, before)
        plane = pltpu.roll(plane, shift, 1) if shift else plane
        scratch[pl.ds(groups + i, count - 1, stride=groups), :] = plane


def unpack_modes(blocks, out, modes, skip):
    groups = LANES // modes
    rows = out.shape[0] // groups
    wide = out.shape[1]
    placed = []
    for index, packed in blocks:
        placed.append((index, pltpu.roll(packed, index * modes, 1)))
    group = lane_group((placed[0][1].shape[0], LANES), modes)
    for s in range(groups):
        total = None
        for index, packed in placed:
            shift = modes * (s + 1) % LANES
            value = pltpu.roll(packed, shift, 1) if shift else packed
            value = jnp.where(group == index, value, 0.0)
            total = value if total is None else total + value
        out[pl.ds(s, rows, stride=groups), :] = total[skip // groups :, :wide]


def load_pieces(plan, refs, bank, sems, meta):
    waits = []
    for i, (row, rows, start, sources) in enumerate(plan):
        target = bank.at[pl.ds(row, rows), :]

        def copy_of(source):
            return pltpu.make_async_copy(refs[source].at[pl.ds(start, rows), :], target, sems.at[i])

        if len(sources) == 1:
            copy_of(sources[0]).start()
        else:
            for choice, source in enumerate(sources):

                @pl.when(meta[MIDDLE_FLAG] == choice)
                def _():
                    copy_of(source).start()

        waits.append(copy_of(sources[0]))
    return waits


def first_lag(meta, part, count, lags):
    if isinstance(part, int):
        return part * lags
    here, index = part
    side = meta[GRP] if here else 1 - meta[GRP]
    return pl.multiple_of((side * (count // 2) + index) * lags, 16)


def stage_kernel(behind, series, ahead, out, sems):
    days = series.shape[0]
    copies = [
        pltpu.make_async_copy(behind, out.at[pl.ds(0, HALO), :], sems.at[0]),
        pltpu.make_async_copy(series, out.at[pl.ds(HALO, days), :], sems.at[1]),
        pltpu.make_async_copy(ahead, out.at[pl.ds(HALO + days, HALO), :], sems.at[2]),
    ]
    for copy in copies:
        copy.start()
    for copy in copies:
        copy.wait()


def project_kernel(plan, parts, first_slot, count, modes, n_refs, finish, *refs):
    meta, source = refs[:2]
    pieces = refs[2 : 2 + n_refs]
    at = 2 + n_refs
    acc_in = None
    if first_slot > 0:
        acc_in = refs[at]
        at += 2
    out, bank, acc, scratch, sems = refs[at:]
    lags = WIDE // modes
    for copy in load_pieces(plan, pieces, bank, sems, meta):
        copy.wait()
    rows = acc.shape[0]
    for slot, part in enumerate(parts, first_slot):
        term = lax.dot_general(
            source[pl.ds(first_lag(meta, part, count, lags), rows), :],
            bank[slot * WIDE : (slot + 1) * WIDE, :],
            (((1,), (1,)), ((), ())),
            preferred_element_type=jnp.float32,
        )
        if slot > first_slot:
            acc[...] += term
        elif first_slot > 0:
            acc[...] = acc_in[...] + term
        else:
            acc[...] = term
    if finish:
        out[...] = pack_skewed(acc, scratch, rows - lags, modes)
    else:
        out[...] = acc[...]


def rebuild_kernel(parts, count, modes, n_sums, n_old, has_in, last, order, total_days, width, days, *refs):
    meta = refs[0]
    n_blocks = len(n_sums)
    at = 1
    sums = []
    for size in n_sums:
        sums.append(refs[at : at + size])
        at += size
    banks = refs[at : at + n_blocks]
    at += n_blocks
    olds = refs[at : at + n_old]
    at += n_old
    rec_in = None
    if has_in:
        rec_in = refs[at]
        at += 1
    rec_out = refs[at]
    at += 1
    if last:
        pcs_out = refs[at]
        at += 1
        stacked, scratch, done, pcs_done, sems = refs[at:]
    else:
        packed_out = refs[at : at + n_blocks]
        at += n_blocks
        stacked, scratch = refs[at:]
    lags = WIDE // modes
    groups = LANES // modes
    per_block = len(parts) // n_blocks
    cells = banks[0].shape[1]
    values = []
    for block in range(n_blocks):
        level = [ref[...] for ref in sums[block]]
        while len(level) > 1:
            level = [level[i] + level[i + 1] for i in range(0, len(level), 2)]
        packed = level[0]
        day = groups * lax.broadcasted_iota(jnp.int32, packed.shape, 0)
        day = day + (groups - 1 - lane_group(packed.shape, modes)) + meta[DAY] - HALO
        packed = jnp.where((day >= 0) & (day <= total_days - width), packed, 0.0)
        values.append(packed)
        if not last:
            packed_out[block][...] = packed
        narrow = packed.astype(jnp.bfloat16).astype(jnp.float32)
        spread_skewed(narrow, scratch, modes)
        for index in range(per_block):
            slot = block * per_block + index
            lag = first_lag(meta, parts[slot], count, lags)
            low = pl.multiple_of(HALO - lag, 8)
            high = pl.multiple_of(HALO - groups - lag, 8)
            start = slot * WIDE
            stacked[:, start : start + LANES] = scratch[pl.ds(low, days), :].astype(jnp.bfloat16)
            stacked[:, start + LANES : start + WIDE] = scratch[pl.ds(high, days), :].astype(jnp.bfloat16)
    if last:
        day = meta[DAY] + lax.broadcasted_iota(jnp.int32, (days, 1), 0)
        windows = jnp.minimum(day, total_days - width) - jnp.maximum(0, day - width + 1) + 1
        scale = 1.0 / windows.astype(jnp.float32)
    copies = []
    depth = per_block * WIDE
    for i, start in enumerate(range(0, cells, TILE)):
        tile = slice(start, start + TILE)
        total = rec_in[:, tile] if has_in else None
        for block, bank in enumerate(banks):
            term = jnp.dot(
                stacked[:, block * depth : (block + 1) * depth],
                bank[:, tile],
                preferred_element_type=jnp.float32,
            )
            total = term if total is None else total + term
        if last:
            done[:, tile] = total * scale
            copies.append(pltpu.make_async_copy(done.at[:, tile], rec_out.at[:, tile], sems.at[i]))
            copies[-1].start()
        else:
            rec_out[:, tile] = total
    if last:
        values = [ref[...] for ref in olds] + values
        unpack_modes([(meta[BLOCKS + i], v) for i, v in zip(order, values)], pcs_done, modes, HALO)
        copies.append(pltpu.make_async_copy(pcs_done, pcs_out, sems.at[len(copies)]))
        copies[-1].start()
        for copy in copies:
            copy.wait()


def space(kind):
    return pl.BlockSpec(memory_space=kind)


def pinned(x):
    return pltpu.with_memory_space_constraint(x, pltpu.VMEM)


def flatten(pieces, row):
    arrays, plan = [], []
    for choices in pieces:
        ids = tuple(range(len(arrays), len(arrays) + len(choices)))
        arrays.extend(choices)
        rows = choices[0].shape[0]
        plan.append((row, rows, 0, ids))
        row += rows
    return plan, arrays


def stage(behind, series, ahead):
    days, cells = series.shape
    return pl.pallas_call(
        stage_kernel,
        out_shape=pltpu.VMEM((days + 2 * HALO, cells), jnp.bfloat16),
        in_specs=[space(pltpu.HBM)] * 3,
        out_specs=space(pltpu.VMEM),
        scratch_shapes=[pltpu.SemaphoreType.DMA((3,))],
        compiler_params=pltpu.CompilerParams(vmem_limit_bytes=VMEM_BYTES),
        name="stage",
    )(behind, series, ahead)


def project(meta, source, pieces, parts, modes, width, before=None, finish=True):
    cells = source.shape[1]
    lags = WIDE // modes
    slots = width // lags
    first_slot = slots - len(parts) if before else 0
    plan, arrays = flatten(pieces, first_slot * WIDE)
    long = source.shape[0] - HALO
    rows = long + lags
    if finish:
        out = jax.ShapeDtypeStruct((long * modes // LANES, LANES), jnp.float32)
    else:
        out = pltpu.VMEM((rows, WIDE), jnp.float32)
    before = [pinned(x) for x in before] if before else []
    return pl.pallas_call(
        functools.partial(project_kernel, plan, parts, first_slot, slots, modes, len(arrays), finish),
        out_shape=(out, pltpu.VMEM((slots * WIDE, cells), jnp.bfloat16)),
        in_specs=[space(pltpu.SMEM), space(pltpu.VMEM)]
        + [space(pltpu.HBM)] * len(arrays)
        + [space(pltpu.VMEM)] * len(before),
        out_specs=(space(pltpu.VMEM), space(pltpu.VMEM)),
        scratch_shapes=[
            pltpu.VMEM((rows, WIDE), jnp.float32),
            pltpu.VMEM((rows - lags // 2, LANES), jnp.float32),
            pltpu.SemaphoreType.DMA((len(plan),)),
        ],
        input_output_aliases={3 + len(arrays): 1} if before else {},
        compiler_params=pltpu.CompilerParams(vmem_limit_bytes=VMEM_BYTES),
        cost_estimate=pl.CostEstimate(
            flops=2 * rows * len(parts) * WIDE * cells,
            bytes_accessed=2 * cells * len(parts) * WIDE,
            transcendentals=0,
        ),
        name="project",
    )(meta, pinned(source), *arrays, *before)


def rebuild(meta, blocks, modes, width, days, total_days, all_modes, so_far=None, old=(), last=False):
    lags = WIDE // modes
    banks = [pinned(block[2]) for block in blocks]
    parts = [part for block in blocks for part in block[3]]
    sums = [value for block in blocks for value in block[1]]
    cells = banks[0].shape[1]
    packed = sums[0].shape
    has_in = so_far is not None
    olds = [value for _, value in old] if last else []
    order = tuple([index for index, _ in old] + [block[0] for block in blocks]) if last else ()
    scratch = [
        pltpu.VMEM((days, len(parts) * WIDE), jnp.bfloat16),
        pltpu.VMEM((days + HALO, LANES), jnp.float32),
    ]
    if last:
        out_shape = [jax.ShapeDtypeStruct((days, cells), jnp.float32)]
        out_shape += [jax.ShapeDtypeStruct((days, all_modes), jnp.float32)]
        out_specs = [space(pltpu.HBM), space(pltpu.HBM)]
        scratch += [
            pltpu.VMEM((days, cells), jnp.float32),
            pltpu.VMEM((days, all_modes), jnp.float32),
            pltpu.SemaphoreType.DMA((cells // TILE + 1,)),
        ]
    else:
        out_shape = [pltpu.VMEM((days, cells), jnp.float32)]
        out_shape += [jax.ShapeDtypeStruct(packed, jnp.float32) for _ in blocks]
        out_specs = [space(pltpu.VMEM)] * len(out_shape)
    before = 1 + len(sums) + len(banks)
    return pl.pallas_call(
        functools.partial(
            rebuild_kernel,
            parts,
            width // lags,
            modes,
            [len(block[1]) for block in blocks],
            len(olds),
            has_in,
            last,
            order,
            total_days,
            width,
            days,
        ),
        out_shape=out_shape,
        in_specs=[space(pltpu.SMEM)] + [space(pltpu.VMEM)] * (len(sums) + len(banks) + len(olds) + has_in),
        out_specs=out_specs,
        scratch_shapes=scratch,
        input_output_aliases={before: 0} if has_in and not last else {},
        compiler_params=pltpu.CompilerParams(vmem_limit_bytes=VMEM_BYTES),
        cost_estimate=pl.CostEstimate(
            flops=2 * days * len(parts) * WIDE * cells,
            bytes_accessed=4 * days * cells,
            transcendentals=0,
        ),
        name="rebuild",
    )(meta, *sums, *banks, *olds, *([pinned(so_far)] if has_in else []))


def exchange(packed):
    size = lax.axis_size("cell")
    return [packed] + [
        lax.ppermute(packed, "cell", [(i, i ^ step) for i in range(size)]) for step in range(1, size)
    ]


def on_device(series, eofs):
    width, modes, cells = eofs.shape
    days = series.shape[0]
    n = lax.axis_size("day")
    total_days = days * n
    day = lax.axis_index("day").astype(jnp.int32)
    grp = lax.axis_index("grp").astype(jnp.int32)
    n_parts = width * modes // WIDE
    bank = eofs.reshape(width * modes, cells)
    behind = lax.ppermute(series[days - HALO :], "day", [(i, i + 1) for i in range(n - 1)])
    ahead = lax.ppermute(series[:HALO], "day", [(i + 1, i) for i in range(n - 1)])
    middle = ((day > 0) & (day < n - 1)).astype(jnp.int32)
    whole = list(range(n_parts))
    shape = dict(modes=modes, width=width)
    rest = dict(days=days, total_days=total_days, all_modes=modes * n)

    if n != 4 or lax.axis_size("grp") != 2 or n_parts != 4:
        every = lax.all_gather(bank, "day", axis=0, tiled=False)
        meta = jnp.stack([day * days, grp, middle] + [jnp.int32(i) for i in range(n)])
        source = stage(behind, series, ahead)
        rec, old = None, []
        for block in range(n):
            pieces = [(every[block],)]
            packed, bank = project(meta, source, pieces, whole, **shape)
            rec, small = rebuild(
                meta, [(block, exchange(packed), bank, whole)], so_far=rec, old=old, last=block == n - 1, **shape, **rest
            )
            old.append((block, small))
        return small, rec

    def table(values):
        return jnp.asarray(values, jnp.int32)[day]

    meta = jnp.stack(
        [day * days, grp, middle, day, table([1, 0, 3, 2]), table([2, 2, 1, 1]), table([3, 3, 0, 0])]
    )
    cuts = 4
    half = width * modes // 2
    size = half // cuts
    first = lax.dynamic_slice_in_dim(bank, grp * half, half, axis=0)
    held = {("own", i): first[i * size : (i + 1) * size] for i in range(cuts)}
    held["behind"], held["ahead"] = behind, ahead
    sent_from = {
        "p1": "own", "p2": "own", "q1": "p2", "q2": "p1", "f": "q2",
        "yp1": "p1", "yp2": "p2", "yq1": "q1", "yq2": "q2", "yf": "f", "h": "yp1", "g": "h",
    }

    def across(array, members):
        return lax.ppermute(
            array,
            ("grp", "day"),
            [(g * n + d, (1 - g) * n + d) for g in (0, 1) for d in members],
        )

    def send(name, array):
        if name == "p1":
            return lax.ppermute(array, "day", PAIRED)
        if name in ("p2", "q2", "h"):
            return lax.ppermute(array, "day", MIDDLE)
        if name in ("q1", "f", "g"):
            return lax.ppermute(array, "day", OUTWARD)
        return across(array, {"yp1": ENDS + MIDS, "yp2": MIDS, "yq1": ENDS, "yq2": MIDS, "yf": ENDS}[name])

    halves = [(True, 0), (True, 1), (False, 0), (False, 1)]
    arrivals = {"a": ("p1",), "b": ("q1", "p2"), "c": ("f", "q2")}
    place = {"own": 0, "a": 1, "b": 2, "c": 3}

    def pieces_of(block, which=range(2 * cuts)):
        if block == "own":
            return [(bank,)]
        picked = []
        for i in which:
            names = arrivals[block] if i < cuts else ["y" + name for name in arrivals[block]]
            if block == "c" and i == 2 * cuts - 1:
                names = ("g", "h")
            picked.append(tuple(held[name, i % cuts] for name in names))
        return picked

    def run(kind, which):
        if kind == "stage":
            held["source"] = stage(held["behind"], series, held["ahead"])
        elif kind == "project":
            source = held["source"]
            if which == "c1":
                held["acc"], held["bank", "c"] = project(
                    meta, source, pieces_of("c", range(6)), halves[:3], finish=False, **shape
                )
            elif which == "c2":
                before = (held["acc"], held["bank", "c"])
                held["packed", "c"], held["bank", "c"] = project(
                    meta, source, pieces_of("c", range(6, 8)), halves[3:], before=before, **shape
                )
            else:
                parts = whole if which == "own" else halves
                held["packed", which], held["bank", which] = project(
                    meta, source, pieces_of(which), parts, **shape
                )
        elif kind == "exchange":
            for i, array in enumerate(exchange(held["packed", which])):
                held["sum", which, i] = array
        else:
            blocks = []
            for block in which:
                sums = [held["sum", block, i] for i in range(lax.axis_size("cell"))]
                parts = whole if block == "own" else halves
                blocks.append((place[block], sums, held["bank", block], parts))
            last = "c" in which
            old = [(place[b], held["old", b]) for b in place if ("old", b) in held]
            done = rebuild(meta, blocks, so_far=held.get("rec"), old=old, last=last, **shape, **rest)
            held["rec"] = done[0]
            if last:
                held["pcs"] = done[1]
            else:
                held.update({("old", block): value for block, value in zip(which, done[1:])})

    tasks = {
        2: [("stage", None), ("project", "own")],
        3: [("exchange", "own")],
        5: [("rebuild", ("own",))],
        7: [("project", "a")],
        8: [("exchange", "a")],
        10: [("rebuild", ("a",))],
        11: [("project", "b")],
        12: [("exchange", "b"), ("project", "c1")],
        13: [("rebuild", ("b",)), ("project", "c2")],
        14: [("exchange", "c")],
        15: [("rebuild", ("c",))],
    }

    lag = 2
    done_at = []
    for slot in range(16):
        sends = []
        if slot < cuts:
            sends += [("p1", slot), ("p2", slot)]
        elif slot < 2 * cuts:
            sends += [("q1", slot - cuts), ("q2", slot - cuts)]
        elif slot < 3 * cuts:
            sends += [("f", slot - 2 * cuts)]
        late = slot - lag
        if 0 <= late < cuts:
            sends += [("yp1", late)]
        elif cuts <= late < 2 * cuts:
            sends += [("yp2", late - cuts), ("yq1", late - cuts)]
        elif 2 * cuts <= late < 3 * cuts - 1:
            sends += [("yq2", late - 2 * cuts), ("yf", late - 2 * cuts)]
        if slot == 2 * cuts:
            sends += [("h", cuts - 1)]
        if slot == 3 * cuts:
            sends = [("g", cuts - 1)] + sends
        if lag <= slot < 3 * cuts + 1:
            keys = [(sent_from[name], i) for name, i in sends] + done_at[slot - lag]
            keys = list(dict.fromkeys(keys))
            values = lax.optimization_barrier(tuple(held[key] for key in keys))
            held.update(zip(keys, values))
        before = dict(held)
        for name, i in sends:
            held[name, i] = send(name, held[sent_from[name], i])
        for task in tasks.get(slot, []):
            run(*task)
        done_at.append([key for key, value in held.items() if before.get(key) is not value])
    return held["pcs"], held["rec"]


def solution(mesh):
    return jax.shard_map(
        on_device,
        mesh=mesh,
        in_specs=(P(("grp", "day"), "cell"), P(None, "day", "cell")),
        out_specs=(P(("grp", "day"), None), P(("grp", "day"), "cell")),
        check_vma=False,
    )
```

```python
import functools

import jax
import jax.numpy as jnp
from jax import lax
from jax.experimental import pallas as pl
from jax.experimental.pallas import tpu as pltpu
from jax.sharding import PartitionSpec as P

LANES = 128
CUTS = (1, 1, 1, 1)
EXTENDED = 1
WIDE = 256
TILE = 512
HALO = 64
VMEM_BYTES = 20 * 1024 * 1024
DAY, GRP, MIDDLE_FLAG, EVEN, BLOCKS = 0, 1, 2, 3, 4

ENDS, MIDS = (0, 3), (1, 2)
PAIRED = ((0, 1), (1, 0), (2, 3), (3, 2))
MIDDLE = ((1, 2), (2, 1))
OUTWARD = ((1, 0), (2, 3))


def lane_group(shape, modes):
    return lax.broadcasted_iota(jnp.int32, shape, len(shape) - 1) // modes


def pack_skewed(acc, scratch, rows, modes):
    groups = LANES // modes
    long = rows + groups
    scratch[...] = acc[:long, :LANES] + acc[groups : long + groups, LANES:]
    count = long // groups
    group = lane_group((count, LANES), modes)
    here = before = None
    for i in range(groups):
        plane = scratch[pl.ds(i, count, stride=groups), :]
        plane = pltpu.roll(plane, modes * (groups - 1 - i), 1) if i < groups - 1 else plane
        stays = group >= groups - 1 - i
        kept, moved = jnp.where(stays, plane, 0.0), jnp.where(stays, 0.0, plane)
        here = kept if here is None else here + kept
        before = moved if before is None else before + moved
    return here[: rows // groups] + before[1:]


def spread_skewed(packed, scratch, modes):
    groups = LANES // modes
    count = packed.shape[0]
    group = lane_group((count - 1, LANES), modes)
    here, before = packed[1:], packed[:-1]
    for i in range(groups):
        shift = modes * (i + 1) % LANES
        plane = jnp.where(group >= groups - 1 - i, here, before)
        plane = pltpu.roll(plane, shift, 1) if shift else plane
        scratch[pl.ds(groups + i, count - 1, stride=groups), :] = plane


def unpack_modes(blocks, out, scratch, modes, skip):
    groups = LANES // modes
    rows = out.shape[1] // groups
    wide = out.shape[0]
    placed = []
    for index, packed in blocks:
        placed.append((index, pltpu.roll(packed, index * modes, 1)))
    group = lane_group((placed[0][1].shape[0], LANES), modes)
    for s in range(groups):
        total = None
        for index, packed in placed:
            shift = modes * (s + 1) % LANES
            value = pltpu.roll(packed, shift, 1) if shift else packed
            value = jnp.where(group == index, value, 0.0)
            total = value if total is None else total + value
        scratch[pl.ds(s, rows, stride=groups), :] = total[skip // groups :]
    out[...] = scratch[: out.shape[1], :].T[:wide]


def load_pieces(plan, refs, bank, sems, meta):
    waits = []
    for i, (row, rows, sources) in enumerate(plan):
        target = bank.at[pl.ds(row, rows), :]

        def copy_of(source):
            ref, start = source
            return pltpu.make_async_copy(refs[ref].at[pl.ds(start, rows), :], target, sems.at[i])

        if len(sources) == 1:
            copy_of(sources[0]).start()
        else:
            for choice, source in enumerate(sources):

                @pl.when(meta[MIDDLE_FLAG] == choice)
                def _():
                    copy_of(source).start()

        waits.append(copy_of(sources[0]))
    return waits


def first_lag(meta, part, count, lags):
    if isinstance(part, int):
        return part * lags
    here, index = part
    side = meta[GRP] if here else 1 - meta[GRP]
    return pl.multiple_of((side * (count // 2) + index) * lags, 16)


def stage_kernel(starts, meta, paired, series, other, out, sems):
    days = series.shape[0]
    places = (pl.ds(0, HALO), pl.ds(HALO + days, HALO))
    middle = pltpu.make_async_copy(series, out.at[pl.ds(HALO, days), :], sems.at[0])
    middle.start()
    waits = [middle]
    for i, (ref, start) in enumerate(zip((paired, other), starts)):
        for even in (0, 1):
            copy = pltpu.make_async_copy(
                ref.at[pl.ds(start, HALO), :], out.at[places[even ^ i], :], sems.at[i + 1]
            )

            @pl.when(meta[EVEN] == even)
            def _():
                copy.start()

        waits.append(copy)
    for copy in waits:
        copy.wait()


def project_kernel(plan, parts, first_slot, count, modes, n_refs, finish, *refs):
    meta, source = refs[:2]
    pieces = refs[2 : 2 + n_refs]
    at = 2 + n_refs
    acc_in = None
    if first_slot > 0:
        acc_in = refs[at]
        at += 2
    out, bank, acc, scratch, sems = refs[at:]
    lags = WIDE // modes
    for copy in load_pieces(plan, pieces, bank, sems, meta):
        copy.wait()
    rows = acc.shape[0]
    for slot, part in enumerate(parts, first_slot):
        term = lax.dot_general(
            source[pl.ds(first_lag(meta, part, count, lags), rows), :],
            bank[slot * WIDE : (slot + 1) * WIDE, :],
            (((1,), (1,)), ((), ())),
            preferred_element_type=jnp.float32,
        )
        if slot > first_slot:
            acc[...] += term
        elif first_slot > 0:
            acc[...] = acc_in[...] + term
        else:
            acc[...] = term
    if finish:
        out[...] = pack_skewed(acc, scratch, rows - lags, modes)
    else:
        out[...] = acc[...]


def rebuild_kernel(parts, count, modes, n_sums, n_old, has_in, last, order, total_days, width, days, *refs):
    meta = refs[0]
    n_blocks = len(n_sums)
    at = 1
    sums = []
    for size in n_sums:
        sums.append(refs[at : at + size])
        at += size
    banks = refs[at : at + n_blocks]
    at += n_blocks
    olds = refs[at : at + n_old]
    at += n_old
    rec_in = None
    if has_in:
        rec_in = refs[at]
        at += 1
    rec_out = refs[at]
    at += 1
    if last:
        pcs_out = refs[at]
        at += 1
        stacked, scratch, done, pcs_done, sems = refs[at:]
    else:
        packed_out = refs[at : at + n_blocks]
        at += n_blocks
        stacked, scratch = refs[at:]
    lags = WIDE // modes
    groups = LANES // modes
    per_block = len(parts) // n_blocks
    cells = banks[0].shape[1]
    values = []
    for block in range(n_blocks):
        level = [ref[...] for ref in sums[block]]
        if len(level) == 1:
            level = [level[0][i] for i in range(level[0].shape[0])]
        while len(level) > 1:
            level = [level[i] + level[i + 1] for i in range(0, len(level), 2)]
        packed = level[0]
        day = groups * lax.broadcasted_iota(jnp.int32, packed.shape, 0)
        day = day + (groups - 1 - lane_group(packed.shape, modes)) + meta[DAY] - HALO
        packed = jnp.where((day >= 0) & (day <= total_days - width), packed, 0.0)
        values.append(packed)
        if not last:
            packed_out[block][...] = packed
        narrow = packed.astype(jnp.bfloat16).astype(jnp.float32)
        spread_skewed(narrow, scratch, modes)
        for index in range(per_block):
            slot = block * per_block + index
            lag = first_lag(meta, parts[slot], count, lags)
            low = pl.multiple_of(HALO - lag, 8)
            high = pl.multiple_of(HALO - groups - lag, 8)
            start = slot * WIDE
            stacked[:, start : start + LANES] = scratch[pl.ds(low, days), :].astype(jnp.bfloat16)
            stacked[:, start + LANES : start + WIDE] = scratch[pl.ds(high, days), :].astype(jnp.bfloat16)
    if last:
        day = meta[DAY] + lax.broadcasted_iota(jnp.int32, (days, 1), 0)
        windows = jnp.minimum(day, total_days - width) - jnp.maximum(0, day - width + 1) + 1
        scale = 1.0 / windows.astype(jnp.float32)
    copies = []
    depth = per_block * WIDE
    for i, start in enumerate(range(0, cells, TILE)):
        tile = slice(start, start + TILE)
        total = rec_in[:, tile] if has_in else None
        for block, bank in enumerate(banks):
            term = jnp.dot(
                stacked[:, block * depth : (block + 1) * depth],
                bank[:, tile],
                preferred_element_type=jnp.float32,
            )
            total = term if total is None else total + term
        if last:
            done[:, tile] = total * scale
            copies.append(pltpu.make_async_copy(done.at[:, tile], rec_out.at[:, tile], sems.at[i]))
            copies[-1].start()
        else:
            rec_out[:, tile] = total
    if last:
        values = [ref[...] for ref in olds] + values
        unpack_modes([(meta[BLOCKS + i], v) for i, v in zip(order, values)], pcs_done, scratch, modes, HALO)
        copies.append(pltpu.make_async_copy(pcs_done, pcs_out, sems.at[len(copies)]))
        copies[-1].start()
        for copy in copies:
            copy.wait()


def space(kind):
    return pl.BlockSpec(memory_space=kind)


def pinned(x):
    return pltpu.with_memory_space_constraint(x, pltpu.VMEM)


def left(x):
    return pltpu.with_memory_space_constraint(x, pltpu.HBM)


def flatten(pieces, row):
    arrays, plan = [], []
    for rows, choices in pieces:
        sources = []
        for array, start in choices:
            same = [i for i, other in enumerate(arrays) if other is array]
            if not same:
                arrays.append(array)
            sources.append((same[0] if same else len(arrays) - 1, start))
        plan.append((row, rows, sources))
        row += rows
    return plan, arrays


def stage(meta, paired, series, other, starts=(0, 0)):
    days, cells = series.shape
    return pl.pallas_call(
        functools.partial(stage_kernel, starts),
        out_shape=pltpu.VMEM((days + 2 * HALO, cells), jnp.bfloat16),
        in_specs=[space(pltpu.SMEM)] + [space(pltpu.HBM)] * 3,
        out_specs=space(pltpu.VMEM),
        scratch_shapes=[pltpu.SemaphoreType.DMA((3,))],
        compiler_params=pltpu.CompilerParams(vmem_limit_bytes=VMEM_BYTES),
        name="stage",
    )(meta, paired, series, other)


def cut_kernel(pieces, extended, half, meta, bank, series, *refs):
    outs, sems = refs[:-1], refs[-1]
    days = series.shape[0]
    copies = []
    for i, out in enumerate(outs):
        edge = i - extended if extended <= i < extended + 2 else None
        start, size = pieces[i if i <= extended else i - 1]
        first = pl.multiple_of(meta[GRP] * half + start, 16)
        copies.append(
            pltpu.make_async_copy(bank.at[pl.ds(first, size), :], out.at[pl.ds(0, size), :], sems.at[i])
        )
        copies[-1].start()
        if edge is not None:
            tail = meta[EVEN] if edge == 0 else (meta[DAY] == days).astype(jnp.int32)
            first = pl.multiple_of(tail * (days - HALO), 16)
            copies.append(
                pltpu.make_async_copy(
                    series.at[pl.ds(first, HALO), :], out.at[pl.ds(size, HALO), :], sems.at[len(outs) + edge]
                )
            )
            copies[-1].start()
    for copy in copies:
        copy.wait()


def cut(meta, bank, series, pieces, extended, half):
    cells = bank.shape[1]
    rows = [size for _, size in pieces]
    rows = rows[:extended] + [rows[extended] + HALO] * 2 + rows[extended + 1 :]
    return pl.pallas_call(
        functools.partial(cut_kernel, pieces, extended, half),
        out_shape=[jax.ShapeDtypeStruct((size, cells), bank.dtype) for size in rows],
        in_specs=[space(pltpu.SMEM)] + [space(pltpu.HBM)] * 2,
        out_specs=[space(pltpu.HBM)] * len(rows),
        scratch_shapes=[pltpu.SemaphoreType.DMA((len(rows) + 2,))],
        compiler_params=pltpu.CompilerParams(vmem_limit_bytes=VMEM_BYTES),
        name="cut",
    )(meta, left(bank), left(series))


def trim_kernel(*refs):
    sems = refs[-1]
    count = len(refs) // 2
    copies = []
    for i in range(count):
        out = refs[count + i]
        copies.append(pltpu.make_async_copy(refs[i].at[pl.ds(0, out.shape[0]), :], out, sems.at[i]))
        copies[-1].start()
    for copy in copies:
        copy.wait()


def trim(arrays, rows):
    return pl.pallas_call(
        trim_kernel,
        out_shape=[jax.ShapeDtypeStruct((rows, x.shape[1]), x.dtype) for x in arrays],
        in_specs=[space(pltpu.HBM)] * len(arrays),
        out_specs=[space(pltpu.HBM)] * len(arrays),
        scratch_shapes=[pltpu.SemaphoreType.DMA((len(arrays),))],
        compiler_params=pltpu.CompilerParams(vmem_limit_bytes=VMEM_BYTES),
        name="trim",
    )(*arrays)


def project(meta, source, pieces, parts, modes, width, before=None, finish=True):
    cells = source.shape[1]
    lags = WIDE // modes
    slots = width // lags
    first_slot = slots - len(parts) if before else 0
    plan, arrays = flatten(pieces, first_slot * WIDE)
    long = source.shape[0] - HALO
    rows = long + lags
    if finish:
        out = jax.ShapeDtypeStruct((long * modes // LANES, LANES), jnp.float32)
    else:
        out = pltpu.VMEM((rows, WIDE), jnp.float32)
    before = [pinned(x) for x in before] if before else []
    return pl.pallas_call(
        functools.partial(project_kernel, plan, parts, first_slot, slots, modes, len(arrays), finish),
        out_shape=(out, pltpu.VMEM((slots * WIDE, cells), jnp.bfloat16)),
        in_specs=[space(pltpu.SMEM), space(pltpu.VMEM)]
        + [space(pltpu.HBM)] * len(arrays)
        + [space(pltpu.VMEM)] * len(before),
        out_specs=(space(pltpu.VMEM), space(pltpu.VMEM)),
        scratch_shapes=[
            pltpu.VMEM((rows, WIDE), jnp.float32),
            pltpu.VMEM((rows - lags // 2, LANES), jnp.float32),
            pltpu.SemaphoreType.DMA((len(plan),)),
        ],
        input_output_aliases={3 + len(arrays): 1} if before else {},
        compiler_params=pltpu.CompilerParams(vmem_limit_bytes=VMEM_BYTES),
        cost_estimate=pl.CostEstimate(
            flops=2 * rows * len(parts) * WIDE * cells,
            bytes_accessed=2 * cells * len(parts) * WIDE,
            transcendentals=0,
        ),
        name="project",
    )(meta, pinned(source), *arrays, *before)


def rebuild(meta, blocks, modes, width, days, total_days, all_modes, so_far=None, old=(), last=False):
    lags = WIDE // modes
    banks = [pinned(block[2]) for block in blocks]
    parts = [part for block in blocks for part in block[3]]
    sums = [value for block in blocks for value in block[1]]
    cells = banks[0].shape[1]
    packed = sums[0].shape[-2:]
    has_in = so_far is not None
    olds = [value for _, value in old] if last else []
    order = tuple([index for index, _ in old] + [block[0] for block in blocks]) if last else ()
    scratch = [
        pltpu.VMEM((days, len(parts) * WIDE), jnp.bfloat16),
        pltpu.VMEM((days + HALO, LANES), jnp.float32),
    ]
    if last:
        out_shape = [jax.ShapeDtypeStruct((days, cells), jnp.float32)]
        out_shape += [jax.ShapeDtypeStruct((all_modes, days), jnp.float32)]
        out_specs = [space(pltpu.HBM), space(pltpu.HBM)]
        scratch += [
            pltpu.VMEM((days, cells), jnp.float32),
            pltpu.VMEM((all_modes, days), jnp.float32),
            pltpu.SemaphoreType.DMA((cells // TILE + 1,)),
        ]
    else:
        out_shape = [pltpu.VMEM((days, cells), jnp.float32)]
        out_shape += [jax.ShapeDtypeStruct(packed, jnp.float32) for _ in blocks]
        out_specs = [space(pltpu.VMEM)] * len(out_shape)
    before = 1 + len(sums) + len(banks)
    return pl.pallas_call(
        functools.partial(
            rebuild_kernel,
            parts,
            width // lags,
            modes,
            [len(block[1]) for block in blocks],
            len(olds),
            has_in,
            last,
            order,
            total_days,
            width,
            days,
        ),
        out_shape=out_shape,
        in_specs=[space(pltpu.SMEM)] + [space(pltpu.VMEM)] * (len(sums) + len(banks) + len(olds) + has_in),
        out_specs=out_specs,
        scratch_shapes=scratch,
        input_output_aliases={before: 0} if has_in and not last else {},
        compiler_params=pltpu.CompilerParams(vmem_limit_bytes=VMEM_BYTES),
        cost_estimate=pl.CostEstimate(
            flops=2 * days * len(parts) * WIDE * cells,
            bytes_accessed=4 * days * cells,
            transcendentals=0,
        ),
        name="rebuild",
    )(meta, *sums, *banks, *olds, *([pinned(so_far)] if has_in else []))


def exchange(packed):
    size = lax.axis_size("cell")
    return [packed] + [
        lax.ppermute(packed, "cell", [(i, i ^ step) for i in range(size)]) for step in range(1, size)
    ]


def on_device(series, eofs):
    width, modes, cells = eofs.shape
    days = series.shape[0]
    n = lax.axis_size("day")
    total_days = days * n
    day = lax.axis_index("day").astype(jnp.int32)
    grp = lax.axis_index("grp").astype(jnp.int32)
    n_parts = width * modes // WIDE
    bank = eofs.reshape(width * modes, cells)

    middle = ((day > 0) & (day < n - 1)).astype(jnp.int32)
    whole = list(range(n_parts))
    shape = dict(modes=modes, width=width)
    rest = dict(days=days, total_days=total_days, all_modes=modes * n)

    if n != 4 or lax.axis_size("grp") != 2 or n_parts != 4:
        every = lax.all_gather(bank, "day", axis=0, tiled=False)
        meta = jnp.stack([day * days, grp, middle, 1 - day % 2] + [jnp.int32(i) for i in range(n)])
        behind = lax.ppermute(series[days - HALO :], "day", [(i, i + 1) for i in range(n - 1)])
        ahead = lax.ppermute(series[:HALO], "day", [(i + 1, i) for i in range(n - 1)])
        even = day % 2 == 0
        source = stage(meta, jnp.where(even, ahead, behind), series, jnp.where(even, behind, ahead))
        rec, old = None, []
        for block in range(n):
            pieces = [(width * modes, [(every[block], 0)])]
            packed, bank = project(meta, source, pieces, whole, **shape)
            rec, small = rebuild(
                meta, [(block, exchange(packed), bank, whole)], so_far=rec, old=old, last=block == n - 1, **shape, **rest
            )
            old.append((block, small))
        return small.T, rec

    entry = lax.broadcasted_iota(jnp.int32, (8,), 0)
    meta = jnp.zeros((8,), jnp.int32)
    low = day // 2
    for i, value in enumerate([day * days, grp, middle, 1 - day % 2, day, day + 1 - 2 * (day % 2), 2 - low, 3 - 3 * low]):
        meta = jnp.where(entry == i, value, meta)
    half = width * modes // 2
    cuts = CUTS
    pieces, row = [], 0
    for size in cuts:
        pieces.append((row * half // sum(cuts), size * half // sum(cuts)))
        row += size
    held = {}
    parts_out = cut(meta, bank, series, pieces, EXTENDED, half)
    for i in range(len(pieces)):
        held["own", i] = parts_out[i if i <= EXTENDED else i + 1]
    extended = {"p1": parts_out[EXTENDED], "p2": parts_out[EXTENDED + 1]}
    n_pieces = len(pieces)
    last_piece = n_pieces - 1
    sent_from = {
        "p1": "own", "p2": "own", "q1": "p2", "q2": "p1", "f": "q2",
        "yp1": "p1", "yp2": "p2", "yq1": "q1", "yq2": "q2", "yf": "f", "h": "yp1", "g": "h",
    }

    def across(array, members):
        return lax.ppermute(
            array,
            ("grp", "day"),
            [(g * n + d, (1 - g) * n + d) for g in (0, 1) for d in members],
        )

    def send(name, array):
        if name == "p1":
            return lax.ppermute(array, "day", PAIRED)
        if name in ("p2", "q2", "h"):
            return lax.ppermute(array, "day", MIDDLE)
        if name in ("q1", "f", "g"):
            return lax.ppermute(array, "day", OUTWARD)
        return across(array, {"yp1": ENDS + MIDS, "yp2": MIDS, "yq1": ENDS, "yq2": MIDS, "yf": ENDS}[name])

    halves = [(True, 0), (True, 1), (False, 0), (False, 1)]
    arrivals = {"a": ("p1",), "b": ("q1", "p2"), "c": ("f", "q2")}
    place = {"own": 0, "a": 1, "b": 2, "c": 3}

    def pieces_of(block, which=range(4)):
        if block == "own":
            return [(width * modes, [(bank, 0)])]
        names = arrivals[block]
        picked = []
        for side in ("", "y"):
            for i, (start, size) in enumerate(pieces):
                ours = [side + name for name in names]
                if block == "c" and side == "y":
                    ours = ["g" if i == last_piece else "yf", "h"]
                choices = [held[name, i] for name in ours]
                for chunk in range(half // WIDE):
                    first = max(start, chunk * WIDE)
                    end = min(start + size, (chunk + 1) * WIDE)
                    if first < end and (side == "y") * (half // WIDE) + chunk in which:
                        picked.append((end - first, [(array, first - start) for array in choices]))
        return picked

    def run(kind, which):
        if kind == "stage":
            starts = (pieces[EXTENDED][1],) * 2
            held["source"] = stage(meta, held["long", "p1"], series, held["long", "p2"], starts)
        elif kind == "project":
            source = held["source"]
            if which == "c1":
                held["acc"], held["bank", "c"] = project(
                    meta, source, pieces_of("c", (0, 1)), halves[:2], finish=False, **shape
                )
            elif which == "c2":
                before = (held["acc"], held["bank", "c"])
                held["packed", "c"], held["bank", "c"] = project(
                    meta, source, pieces_of("c", (2, 3)), halves[2:], before=before, **shape
                )
            else:
                parts = whole if which == "own" else halves
                held["packed", which], held["bank", which] = project(
                    meta, source, pieces_of(which), parts, **shape
                )
        elif kind == "exchange":
            if which == "c":
                held["sum", which] = exchange(held["packed", which])
            else:
                held["sum", which] = [lax.all_gather(held["packed", which], "cell", axis=0)]
        else:
            blocks = []
            for block in which:
                sums = held["sum", block]
                parts = whole if block == "own" else halves
                blocks.append((place[block], sums, held["bank", block], parts))
            last = "c" in which
            old = [(place[b], held["old", b]) for b in place if ("old", b) in held]
            done = rebuild(meta, blocks, so_far=held.get("rec"), old=old, last=last, **shape, **rest)
            held["rec"] = done[0]
            if last:
                held["pcs"] = done[1]
            else:
                held.update({("old", block): value for block, value in zip(which, done[1:])})

    tasks = {
        3: [("stage", None), ("project", "own")],
        4: [("exchange", "own")],
        5: [("rebuild", ("own",))],
        7: [("project", "a")],
        8: [("exchange", "a")],
        13: [("project", "b"), ("exchange", "b"), ("project", "c1"), ("rebuild", ("a",))],
        14: [("project", "c2")],
        15: [("exchange", "c"), ("rebuild", ("b",))],
        16: [("rebuild", ("c",))],
    }
    lag = 2
    along = [[("p1", i), ("p2", i)] for i in range(n_pieces)]
    along += [[("q1", i), ("q2", i)] for i in range(n_pieces)]
    along += [[("f", i), ("h", (i - 1) % n_pieces)] for i in range(n_pieces)]
    swaps = [[("yp1", i)] for i in range(n_pieces)]
    swaps += [[("yp2", i), ("yq1", i)] for i in range(n_pieces)]
    swaps += [[("yf", i)] for i in range(last_piece)]
    along.append([("g", last_piece)])
    last_slot = len(along) - 1

    done_at = []
    for slot in range(last_slot + 6):
        sends = list(along[slot]) if slot <= last_slot else []
        if 0 <= slot - lag < len(swaps):
            sends += swaps[slot - lag]
        if lag <= slot <= last_slot:
            keys = [(sent_from[name], i) for name, i in sends] + done_at[slot - lag]
            for kind, which in tasks.get(slot, []):
                if kind == "exchange":
                    keys.append(("packed", which))
                if kind == "rebuild":
                    keys += [("bank", block) for block in which]
            keys = [key for key in dict.fromkeys(keys) if key in held]
            values = lax.optimization_barrier(tuple(held[key] for key in keys))
            held.update(zip(keys, values))
        before = dict(held)
        if slot == EXTENDED + lag:
            long = [held["long", name] for name in ("p1", "p2")]
            held["p1", EXTENDED], held["p2", EXTENDED] = trim(long, pieces[EXTENDED][1])
        for name, i in sends:
            if i == EXTENDED and name in extended:
                held["long", name] = send(name, extended[name])
                continue
            held[name, i] = send(name, held[sent_from[name], i])
        for task in tasks.get(slot, []):
            run(*task)
        done_at.append([key for key, value in held.items() if before.get(key) is not value])
    return held["pcs"].T, held["rec"]


def solution(mesh):
    return jax.shard_map(
        on_device,
        mesh=mesh,
        in_specs=(P(("grp", "day"), "cell"), P(None, "day", "cell")),
        out_specs=(P(("grp", "day"), None), P(("grp", "day"), "cell")),
        check_vma=False,
    )
```

```python
import functools

import jax
import jax.numpy as jnp
from jax import lax
from jax.experimental import pallas as pl
from jax.experimental.pallas import tpu as pltpu
from jax.sharding import PartitionSpec as P

LANES = 128
CUTS = (1, 1, 1, 1)
EXTENDED = 1
WIDE = 256
TILE = 512
HALO = 64
VMEM_BYTES = 20 * 1024 * 1024
DAY, GRP, MIDDLE_FLAG, EVEN, BLOCKS = 0, 1, 2, 3, 4

ENDS, MIDS = (0, 3), (1, 2)
PAIRED = ((0, 1), (1, 0), (2, 3), (3, 2))
MIDDLE = ((1, 2), (2, 1))
OUTWARD = ((1, 0), (2, 3))


def lane_group(shape, modes):
    return lax.broadcasted_iota(jnp.int32, shape, len(shape) - 1) // modes


def pack_skewed(acc, scratch, rows, modes):
    groups = LANES // modes
    long = rows + groups
    scratch[...] = acc[:long, :LANES] + acc[groups : long + groups, LANES:]
    count = long // groups
    group = lane_group((count, LANES), modes)
    here = before = None
    for i in range(groups):
        plane = scratch[pl.ds(i, count, stride=groups), :]
        plane = pltpu.roll(plane, modes * (groups - 1 - i), 1) if i < groups - 1 else plane
        stays = group >= groups - 1 - i
        kept, moved = jnp.where(stays, plane, 0.0), jnp.where(stays, 0.0, plane)
        here = kept if here is None else here + kept
        before = moved if before is None else before + moved
    return here[: rows // groups] + before[1:]


def spread_skewed(packed, scratch, modes):
    groups = LANES // modes
    count = packed.shape[0]
    group = lane_group((count - 1, LANES), modes)
    here, before = packed[1:], packed[:-1]
    for i in range(groups):
        shift = modes * (i + 1) % LANES
        plane = jnp.where(group >= groups - 1 - i, here, before)
        plane = pltpu.roll(plane, shift, 1) if shift else plane
        scratch[pl.ds(groups + i, count - 1, stride=groups), :] = plane


def unpack_modes(blocks, out, scratch, modes, skip):
    groups = LANES // modes
    rows = out.shape[1] // groups
    wide = out.shape[0]
    placed = []
    for index, packed in blocks:
        placed.append((index, pltpu.roll(packed, index * modes, 1)))
    group = lane_group((placed[0][1].shape[0], LANES), modes)
    for s in range(groups):
        total = None
        for index, packed in placed:
            shift = modes * (s + 1) % LANES
            value = pltpu.roll(packed, shift, 1) if shift else packed
            value = jnp.where(group == index, value, 0.0)
            total = value if total is None else total + value
        scratch[pl.ds(s, rows, stride=groups), :] = total[skip // groups :]
    out[...] = scratch[: out.shape[1], :].T[:wide]


def load_pieces(plan, refs, bank, sems, meta):
    waits = []
    for i, (row, rows, sources) in enumerate(plan):
        target = bank.at[pl.ds(row, rows), :]

        def copy_of(source):
            ref, start = source
            return pltpu.make_async_copy(refs[ref].at[pl.ds(start, rows), :], target, sems.at[i])

        if len(sources) == 1:
            copy_of(sources[0]).start()
        else:
            for choice, source in enumerate(sources):

                @pl.when(meta[MIDDLE_FLAG] == choice)
                def _():
                    copy_of(source).start()

        waits.append(copy_of(sources[0]))
    return waits


def first_lag(meta, part, count, lags):
    if isinstance(part, int):
        return part * lags
    here, index = part
    side = meta[GRP] if here else 1 - meta[GRP]
    return pl.multiple_of((side * (count // 2) + index) * lags, 16)


def stage_kernel(starts, meta, paired, series, other, out, sems):
    days = series.shape[0]
    places = (pl.ds(0, HALO), pl.ds(HALO + days, HALO))
    middle = pltpu.make_async_copy(series, out.at[pl.ds(HALO, days), :], sems.at[0])
    middle.start()
    waits = [middle]
    for i, (ref, start) in enumerate(zip((paired, other), starts)):
        for even in (0, 1):
            copy = pltpu.make_async_copy(
                ref.at[pl.ds(start, HALO), :], out.at[places[even ^ i], :], sems.at[i + 1]
            )

            @pl.when(meta[EVEN] == even)
            def _():
                copy.start()

        waits.append(copy)
    for copy in waits:
        copy.wait()


def project_kernel(plan, parts, first_slot, count, modes, n_refs, finish, *refs):
    meta, source = refs[:2]
    pieces = refs[2 : 2 + n_refs]
    at = 2 + n_refs
    acc_in = None
    if first_slot > 0:
        acc_in = refs[at]
        at += 2
    out, bank, acc, scratch, sems = refs[at:]
    lags = WIDE // modes
    for copy in load_pieces(plan, pieces, bank, sems, meta):
        copy.wait()
    rows = acc.shape[0]
    for slot, part in enumerate(parts, first_slot):
        term = lax.dot_general(
            source[pl.ds(first_lag(meta, part, count, lags), rows), :],
            bank[slot * WIDE : (slot + 1) * WIDE, :],
            (((1,), (1,)), ((), ())),
            preferred_element_type=jnp.float32,
        )
        if slot > first_slot:
            acc[...] += term
        elif first_slot > 0:
            acc[...] = acc_in[...] + term
        else:
            acc[...] = term
    if finish:
        out[...] = pack_skewed(acc, scratch, rows - lags, modes)
    else:
        out[...] = acc[...]


def rebuild_kernel(parts, count, modes, n_sums, n_old, has_in, last, order, total_days, width, days, *refs):
    meta = refs[0]
    n_blocks = len(n_sums)
    at = 1
    sums = []
    for size in n_sums:
        sums.append(refs[at : at + size])
        at += size
    banks = refs[at : at + n_blocks]
    at += n_blocks
    olds = refs[at : at + n_old]
    at += n_old
    rec_in = None
    if has_in:
        rec_in = refs[at]
        at += 1
    rec_out = refs[at]
    at += 1
    if last:
        pcs_out = refs[at]
        at += 1
        stacked, scratch, done, pcs_done, sems = refs[at:]
    else:
        packed_out = refs[at : at + n_blocks]
        at += n_blocks
        stacked, scratch = refs[at:]
    lags = WIDE // modes
    groups = LANES // modes
    per_block = len(parts) // n_blocks
    cells = banks[0].shape[1]
    values = []
    for block in range(n_blocks):
        level = [ref[...] for ref in sums[block]]
        if len(level) == 1:
            level = [level[0][i] for i in range(level[0].shape[0])]
        while len(level) > 1:
            level = [level[i] + level[i + 1] for i in range(0, len(level), 2)]
        packed = level[0]
        day = groups * lax.broadcasted_iota(jnp.int32, packed.shape, 0)
        day = day + (groups - 1 - lane_group(packed.shape, modes)) + meta[DAY] - HALO
        packed = jnp.where((day >= 0) & (day <= total_days - width), packed, 0.0)
        values.append(packed)
        if not last:
            packed_out[block][...] = packed
        narrow = packed.astype(jnp.bfloat16).astype(jnp.float32)
        spread_skewed(narrow, scratch, modes)
        for index in range(per_block):
            slot = block * per_block + index
            lag = first_lag(meta, parts[slot], count, lags)
            low = pl.multiple_of(HALO - lag, 8)
            high = pl.multiple_of(HALO - groups - lag, 8)
            start = slot * WIDE
            stacked[:, start : start + LANES] = scratch[pl.ds(low, days), :].astype(jnp.bfloat16)
            stacked[:, start + LANES : start + WIDE] = scratch[pl.ds(high, days), :].astype(jnp.bfloat16)
    if last:
        day = meta[DAY] + lax.broadcasted_iota(jnp.int32, (days, 1), 0)
        windows = jnp.minimum(day, total_days - width) - jnp.maximum(0, day - width + 1) + 1
        scale = 1.0 / windows.astype(jnp.float32)
    copies = []
    depth = per_block * WIDE
    for i, start in enumerate(range(0, cells, TILE)):
        tile = slice(start, start + TILE)
        total = rec_in[:, tile] if has_in else None
        for block, bank in enumerate(banks):
            term = jnp.dot(
                stacked[:, block * depth : (block + 1) * depth],
                bank[:, tile],
                preferred_element_type=jnp.float32,
            )
            total = term if total is None else total + term
        if last:
            done[:, tile] = total * scale
            copies.append(pltpu.make_async_copy(done.at[:, tile], rec_out.at[:, tile], sems.at[i]))
            copies[-1].start()
        else:
            rec_out[:, tile] = total
    if last:
        values = [ref[...] for ref in olds] + values
        unpack_modes([(meta[BLOCKS + i], v) for i, v in zip(order, values)], pcs_done, scratch, modes, HALO)
        copies.append(pltpu.make_async_copy(pcs_done, pcs_out, sems.at[len(copies)]))
        copies[-1].start()
        for copy in copies:
            copy.wait()


def space(kind):
    return pl.BlockSpec(memory_space=kind)


def pinned(x):
    return pltpu.with_memory_space_constraint(x, pltpu.VMEM)


def left(x):
    return pltpu.with_memory_space_constraint(x, pltpu.HBM)


def flatten(pieces, row):
    arrays, plan = [], []
    for rows, choices in pieces:
        sources = []
        for array, start in choices:
            same = [i for i, other in enumerate(arrays) if other is array]
            if not same:
                arrays.append(array)
            sources.append((same[0] if same else len(arrays) - 1, start))
        plan.append((row, rows, sources))
        row += rows
    return plan, arrays


def stage(meta, paired, series, other, starts=(0, 0)):
    days, cells = series.shape
    return pl.pallas_call(
        functools.partial(stage_kernel, starts),
        out_shape=pltpu.VMEM((days + 2 * HALO, cells), jnp.bfloat16),
        in_specs=[space(pltpu.SMEM)] + [space(pltpu.HBM)] * 3,
        out_specs=space(pltpu.VMEM),
        scratch_shapes=[pltpu.SemaphoreType.DMA((3,))],
        compiler_params=pltpu.CompilerParams(vmem_limit_bytes=VMEM_BYTES),
        name="stage",
    )(meta, paired, series, other)


def cut_kernel(pieces, extended, half, meta, bank, series, *refs):
    outs, sems = refs[:-1], refs[-1]
    days = series.shape[0]
    copies = []
    for i, out in enumerate(outs):
        edge = i - extended if extended <= i < extended + 2 else None
        start, size = pieces[i if i <= extended else i - 1]
        first = pl.multiple_of(meta[GRP] * half + start, 16)
        copies.append(
            pltpu.make_async_copy(bank.at[pl.ds(first, size), :], out.at[pl.ds(0, size), :], sems.at[i])
        )
        copies[-1].start()
        if edge is not None:
            tail = meta[EVEN] if edge == 0 else (meta[DAY] == days).astype(jnp.int32)
            first = pl.multiple_of(tail * (days - HALO), 16)
            copies.append(
                pltpu.make_async_copy(
                    series.at[pl.ds(first, HALO), :], out.at[pl.ds(size, HALO), :], sems.at[len(outs) + edge]
                )
            )
            copies[-1].start()
    for copy in copies:
        copy.wait()


def cut(meta, bank, series, pieces, extended, half):
    cells = bank.shape[1]
    rows = [size for _, size in pieces]
    rows = rows[:extended] + [rows[extended] + HALO] * 2 + rows[extended + 1 :]
    return pl.pallas_call(
        functools.partial(cut_kernel, pieces, extended, half),
        out_shape=[jax.ShapeDtypeStruct((size, cells), bank.dtype) for size in rows],
        in_specs=[space(pltpu.SMEM)] + [space(pltpu.HBM)] * 2,
        out_specs=[space(pltpu.HBM)] * len(rows),
        scratch_shapes=[pltpu.SemaphoreType.DMA((len(rows) + 2,))],
        compiler_params=pltpu.CompilerParams(vmem_limit_bytes=VMEM_BYTES),
        name="cut",
    )(meta, left(bank), left(series))


def trim_kernel(*refs):
    sems = refs[-1]
    count = len(refs) // 2
    copies = []
    for i in range(count):
        out = refs[count + i]
        copies.append(pltpu.make_async_copy(refs[i].at[pl.ds(0, out.shape[0]), :], out, sems.at[i]))
        copies[-1].start()
    for copy in copies:
        copy.wait()


def trim(arrays, rows):
    return pl.pallas_call(
        trim_kernel,
        out_shape=[jax.ShapeDtypeStruct((rows, x.shape[1]), x.dtype) for x in arrays],
        in_specs=[space(pltpu.HBM)] * len(arrays),
        out_specs=[space(pltpu.HBM)] * len(arrays),
        scratch_shapes=[pltpu.SemaphoreType.DMA((len(arrays),))],
        compiler_params=pltpu.CompilerParams(vmem_limit_bytes=VMEM_BYTES),
        name="trim",
    )(*arrays)


def project(meta, source, pieces, parts, modes, width, before=None, finish=True):
    cells = source.shape[1]
    lags = WIDE // modes
    slots = width // lags
    first_slot = slots - len(parts) if before else 0
    plan, arrays = flatten(pieces, first_slot * WIDE)
    long = source.shape[0] - HALO
    rows = long + lags
    if finish:
        out = jax.ShapeDtypeStruct((long * modes // LANES, LANES), jnp.float32)
    else:
        out = pltpu.VMEM((rows, WIDE), jnp.float32)
    before = [pinned(x) for x in before] if before else []
    return pl.pallas_call(
        functools.partial(project_kernel, plan, parts, first_slot, slots, modes, len(arrays), finish),
        out_shape=(out, pltpu.VMEM((slots * WIDE, cells), jnp.bfloat16)),
        in_specs=[space(pltpu.SMEM), space(pltpu.VMEM)]
        + [space(pltpu.HBM)] * len(arrays)
        + [space(pltpu.VMEM)] * len(before),
        out_specs=(space(pltpu.VMEM), space(pltpu.VMEM)),
        scratch_shapes=[
            pltpu.VMEM((rows, WIDE), jnp.float32),
            pltpu.VMEM((rows - lags // 2, LANES), jnp.float32),
            pltpu.SemaphoreType.DMA((len(plan),)),
        ],
        input_output_aliases={3 + len(arrays): 1} if before else {},
        compiler_params=pltpu.CompilerParams(vmem_limit_bytes=VMEM_BYTES),
        cost_estimate=pl.CostEstimate(
            flops=2 * rows * len(parts) * WIDE * cells,
            bytes_accessed=2 * cells * len(parts) * WIDE,
            transcendentals=0,
        ),
        name="project",
    )(meta, pinned(source), *arrays, *before)


def rebuild(meta, blocks, modes, width, days, total_days, all_modes, so_far=None, old=(), last=False):
    lags = WIDE // modes
    banks = [pinned(block[2]) for block in blocks]
    parts = [part for block in blocks for part in block[3]]
    sums = [value for block in blocks for value in block[1]]
    cells = banks[0].shape[1]
    packed = sums[0].shape[-2:]
    has_in = so_far is not None
    olds = [value for _, value in old] if last else []
    order = tuple([index for index, _ in old] + [block[0] for block in blocks]) if last else ()
    scratch = [
        pltpu.VMEM((days, len(parts) * WIDE), jnp.bfloat16),
        pltpu.VMEM((days + HALO, LANES), jnp.float32),
    ]
    if last:
        out_shape = [jax.ShapeDtypeStruct((days, cells), jnp.float32)]
        out_shape += [jax.ShapeDtypeStruct((all_modes, days), jnp.float32)]
        out_specs = [space(pltpu.HBM), space(pltpu.HBM)]
        scratch += [
            pltpu.VMEM((days, cells), jnp.float32),
            pltpu.VMEM((all_modes, days), jnp.float32),
            pltpu.SemaphoreType.DMA((cells // TILE + 1,)),
        ]
    else:
        out_shape = [pltpu.VMEM((days, cells), jnp.float32)]
        out_shape += [jax.ShapeDtypeStruct(packed, jnp.float32) for _ in blocks]
        out_specs = [space(pltpu.VMEM)] * len(out_shape)
    before = 1 + len(sums) + len(banks)
    return pl.pallas_call(
        functools.partial(
            rebuild_kernel,
            parts,
            width // lags,
            modes,
            [len(block[1]) for block in blocks],
            len(olds),
            has_in,
            last,
            order,
            total_days,
            width,
            days,
        ),
        out_shape=out_shape,
        in_specs=[space(pltpu.SMEM)] + [space(pltpu.VMEM)] * (len(sums) + len(banks) + len(olds) + has_in),
        out_specs=out_specs,
        scratch_shapes=scratch,
        input_output_aliases={before: 0} if has_in and not last else {},
        compiler_params=pltpu.CompilerParams(vmem_limit_bytes=VMEM_BYTES),
        cost_estimate=pl.CostEstimate(
            flops=2 * days * len(parts) * WIDE * cells,
            bytes_accessed=4 * days * cells,
            transcendentals=0,
        ),
        name="rebuild",
    )(meta, *sums, *banks, *olds, *([pinned(so_far)] if has_in else []))


def exchange(packed):
    size = lax.axis_size("cell")
    return [packed] + [
        lax.ppermute(packed, "cell", [(i, i ^ step) for i in range(size)]) for step in range(1, size)
    ]


def on_device(series, eofs):
    width, modes, cells = eofs.shape
    days = series.shape[0]
    n = lax.axis_size("day")
    total_days = days * n
    day = lax.axis_index("day").astype(jnp.int32)
    grp = lax.axis_index("grp").astype(jnp.int32)
    n_parts = width * modes // WIDE
    bank = eofs.reshape(width * modes, cells)

    middle = ((day > 0) & (day < n - 1)).astype(jnp.int32)
    whole = list(range(n_parts))
    shape = dict(modes=modes, width=width)
    rest = dict(days=days, total_days=total_days, all_modes=modes * n)

    if n != 4 or lax.axis_size("grp") != 2 or n_parts != 4:
        every = lax.all_gather(bank, "day", axis=0, tiled=False)
        meta = jnp.stack([day * days, grp, middle, 1 - day % 2] + [jnp.int32(i) for i in range(n)])
        behind = lax.ppermute(series[days - HALO :], "day", [(i, i + 1) for i in range(n - 1)])
        ahead = lax.ppermute(series[:HALO], "day", [(i + 1, i) for i in range(n - 1)])
        even = day % 2 == 0
        source = stage(meta, jnp.where(even, ahead, behind), series, jnp.where(even, behind, ahead))
        rec, old = None, []
        for block in range(n):
            pieces = [(width * modes, [(every[block], 0)])]
            packed, bank = project(meta, source, pieces, whole, **shape)
            rec, small = rebuild(
                meta, [(block, exchange(packed), bank, whole)], so_far=rec, old=old, last=block == n - 1, **shape, **rest
            )
            old.append((block, small))
        return small.T, rec

    entry = lax.broadcasted_iota(jnp.int32, (8,), 0)
    meta = jnp.zeros((8,), jnp.int32)
    low = day // 2
    for i, value in enumerate([day * days, grp, middle, 1 - day % 2, day, day + 1 - 2 * (day % 2), 2 - low, 3 - 3 * low]):
        meta = jnp.where(entry == i, value, meta)
    half = width * modes // 2
    cuts = CUTS
    pieces, row = [], 0
    for size in cuts:
        pieces.append((row * half // sum(cuts), size * half // sum(cuts)))
        row += size
    held = {}
    parts_out = cut(meta, bank, series, pieces, EXTENDED, half)
    for i in range(len(pieces)):
        held["own", i] = parts_out[i if i <= EXTENDED else i + 1]
    extended = {"p1": parts_out[EXTENDED], "p2": parts_out[EXTENDED + 1]}
    n_pieces = len(pieces)
    last_piece = n_pieces - 1
    sent_from = {
        "p1": "own", "p2": "own", "q1": "p2", "q2": "p1", "f": "q2",
        "yp1": "p1", "yp2": "p2", "yq1": "q1", "yq2": "q2", "yf": "f", "h": "yp1", "g": "h",
    }

    def across(array, members):
        return lax.ppermute(
            array,
            ("grp", "day"),
            [(g * n + d, (1 - g) * n + d) for g in (0, 1) for d in members],
        )

    def send(name, array):
        if name == "p1":
            return lax.ppermute(array, "day", PAIRED)
        if name in ("p2", "q2", "h"):
            return lax.ppermute(array, "day", MIDDLE)
        if name in ("q1", "f", "g"):
            return lax.ppermute(array, "day", OUTWARD)
        return across(array, {"yp1": ENDS + MIDS, "yp2": MIDS, "yq1": ENDS, "yq2": MIDS, "yf": ENDS}[name])

    halves = [(True, 0), (True, 1), (False, 0), (False, 1)]
    arrivals = {"a": ("p1",), "b": ("q1", "p2"), "c": ("f", "q2")}
    place = {"own": 0, "a": 1, "b": 2, "c": 3}

    def pieces_of(block, which=range(4)):
        if block == "own":
            return [(width * modes, [(bank, 0)])]
        names = arrivals[block]
        picked = []
        for side in ("", "y"):
            for i, (start, size) in enumerate(pieces):
                ours = [side + name for name in names]
                if block == "c" and side == "y":
                    ours = ["g" if i == last_piece else "yf", "h"]
                choices = [held[name, i] for name in ours]
                for chunk in range(half // WIDE):
                    first = max(start, chunk * WIDE)
                    end = min(start + size, (chunk + 1) * WIDE)
                    if first < end and (side == "y") * (half // WIDE) + chunk in which:
                        picked.append((end - first, [(array, first - start) for array in choices]))
        return picked

    def run(kind, which):
        if kind == "after":
            key, other = which
            held[key], held[other] = lax.optimization_barrier((held[key], held[other]))
        elif kind == "stage":
            starts = (pieces[EXTENDED][1],) * 2
            held["source"] = stage(meta, held["long", "p1"], series, held["long", "p2"], starts)
        elif kind == "project":
            source = held["source"]
            if which == "c1":
                held["acc"], held["bank", "c"] = project(
                    meta, source, pieces_of("c", (0, 1, 2)), halves[:3], finish=False, **shape
                )
            elif which == "c2":
                before = (held["acc"], held["bank", "c"])
                held["packed", "c"], held["bank", "c"] = project(
                    meta, source, pieces_of("c", (3,)), halves[3:], before=before, **shape
                )
            else:
                parts = whole if which == "own" else halves
                held["packed", which], held["bank", which] = project(
                    meta, source, pieces_of(which), parts, **shape
                )
        elif kind == "exchange":
            if which == "c":
                held["sum", which] = exchange(held["packed", which])
            else:
                held["sum", which] = [lax.all_gather(held["packed", which], "cell", axis=0)]
        else:
            blocks = []
            for block in which:
                sums = held["sum", block]
                parts = whole if block == "own" else halves
                blocks.append((place[block], sums, held["bank", block], parts))
            last = "c" in which
            old = [(place[b], held["old", b]) for b in place if ("old", b) in held]
            done = rebuild(meta, blocks, so_far=held.get("rec"), old=old, last=last, **shape, **rest)
            held["rec"] = done[0]
            if last:
                held["pcs"] = done[1]
            else:
                held.update({("old", block): value for block, value in zip(which, done[1:])})

    tasks = {
        3: [("stage", None), ("project", "own")],
        4: [("exchange", "own")],
        5: [("rebuild", ("own",))],
        7: [("project", "a")],
        8: [("exchange", "a")],
        13: [
            ("project", "b"),
            ("after", (("bank", "a"), ("packed", "b"))),
            ("exchange", "b"),
            ("project", "c1"),
            ("rebuild", ("a",)),
        ],
        14: [("project", "c2")],
        15: [("exchange", "c"), ("rebuild", ("b",))],
        16: [("rebuild", ("c",))],
    }
    lag = 2
    along = [[("p1", i), ("p2", i)] for i in range(n_pieces)]
    along += [[("q2", i), ("q1", i)] for i in range(n_pieces)]
    along += [[("f", i), ("h", (i - 1) % n_pieces)] for i in range(n_pieces)]
    swaps = [[("yp1", i)] for i in range(n_pieces)]
    swaps += [[("yp2", i), ("yq1", i)] for i in range(n_pieces)]
    swaps += [[("yf", i)] for i in range(last_piece)]
    along.append([("g", last_piece)])
    last_slot = len(along) - 1

    done_at = []
    for slot in range(last_slot + 6):
        sends = list(along[slot]) if slot <= last_slot else []
        if 0 <= slot - lag < len(swaps):
            sends = swaps[slot - lag] + sends
        if lag <= slot <= last_slot:
            keys = [(sent_from[name], i) for name, i in sends] + done_at[slot - lag]
            for kind, which in tasks.get(slot, []):
                if kind == "exchange":
                    keys.append(("packed", which))
                if kind == "rebuild":
                    keys += [("bank", block) for block in which]
            keys = [key for key in dict.fromkeys(keys) if key in held]
            values = lax.optimization_barrier(tuple(held[key] for key in keys))
            held.update(zip(keys, values))
        before = dict(held)
        if slot == EXTENDED + lag:
            long = [held["long", name] for name in ("p1", "p2")]
            held["p1", EXTENDED], held["p2", EXTENDED] = trim(long, pieces[EXTENDED][1])
        for name, i in sends:
            if i == EXTENDED and name in extended:
                held["long", name] = send(name, extended[name])
                continue
            held[name, i] = send(name, held[sent_from[name], i])
        for task in tasks.get(slot, []):
            run(*task)
        done_at.append([key for key, value in held.items() if before.get(key) is not value])
    return held["pcs"].T, held["rec"]


def solution(mesh):
    return jax.shard_map(
        on_device,
        mesh=mesh,
        in_specs=(P(("grp", "day"), "cell"), P(None, "day", "cell")),
        out_specs=(P(("grp", "day"), None), P(("grp", "day"), "cell")),
        check_vma=False,
    )
```

```python
import functools

import jax
import jax.numpy as jnp
from jax import lax
from jax.experimental import pallas as pl
from jax.experimental.pallas import tpu as pltpu
from jax.sharding import PartitionSpec as P

LANES = 128
CUTS = (1, 1, 1, 1)
EXTENDED = 1
WIDE = 256
TILE = 512
HALO = 64
VMEM_BYTES = 20 * 1024 * 1024
DAY, GRP, MIDDLE_FLAG, EVEN, BLOCKS = 0, 1, 2, 3, 4

ENDS, MIDS = (0, 3), (1, 2)
PAIRED = ((0, 1), (1, 0), (2, 3), (3, 2))
MIDDLE = ((1, 2), (2, 1))
OUTWARD = ((1, 0), (2, 3))


def lane_group(shape, modes):
    return lax.broadcasted_iota(jnp.int32, shape, len(shape) - 1) // modes


def pack_skewed(acc, scratch, rows, modes):
    groups = LANES // modes
    long = rows + groups
    scratch[...] = acc[:long, :LANES] + acc[groups : long + groups, LANES:]
    count = long // groups
    group = lane_group((count, LANES), modes)
    here = before = None
    for i in range(groups):
        plane = scratch[pl.ds(i, count, stride=groups), :]
        plane = pltpu.roll(plane, modes * (groups - 1 - i), 1) if i < groups - 1 else plane
        stays = group >= groups - 1 - i
        kept, moved = jnp.where(stays, plane, 0.0), jnp.where(stays, 0.0, plane)
        here = kept if here is None else here + kept
        before = moved if before is None else before + moved
    return here[: rows // groups] + before[1:]


def spread_skewed(packed, scratch, modes):
    groups = LANES // modes
    count = packed.shape[0]
    group = lane_group((count - 1, LANES), modes)
    here, before = packed[1:], packed[:-1]
    for i in range(groups):
        shift = modes * (i + 1) % LANES
        plane = jnp.where(group >= groups - 1 - i, here, before)
        plane = pltpu.roll(plane, shift, 1) if shift else plane
        scratch[pl.ds(groups + i, count - 1, stride=groups), :] = plane


def unpack_modes(blocks, out, scratch, modes, skip):
    groups = LANES // modes
    rows = out.shape[1] // groups
    wide = out.shape[0]
    placed = []
    for index, packed in blocks:
        placed.append((index, pltpu.roll(packed, index * modes, 1)))
    group = lane_group((placed[0][1].shape[0], LANES), modes)
    for s in range(groups):
        total = None
        for index, packed in placed:
            shift = modes * (s + 1) % LANES
            value = pltpu.roll(packed, shift, 1) if shift else packed
            value = jnp.where(group == index, value, 0.0)
            total = value if total is None else total + value
        scratch[pl.ds(s, rows, stride=groups), :] = total[skip // groups :]
    out[...] = scratch[: out.shape[1], :].T[:wide]


def load_pieces(plan, refs, bank, sems, meta):
    waits = []
    for i, (row, rows, sources) in enumerate(plan):
        target = bank.at[pl.ds(row, rows), :]

        def copy_of(source):
            ref, start = source
            return pltpu.make_async_copy(refs[ref].at[pl.ds(start, rows), :], target, sems.at[i])

        if len(sources) == 1:
            copy_of(sources[0]).start()
        else:
            for choice, source in enumerate(sources):

                @pl.when(meta[MIDDLE_FLAG] == choice)
                def _():
                    copy_of(source).start()

        waits.append(copy_of(sources[0]))
    return waits


def first_lag(meta, part, count, lags):
    if isinstance(part, int):
        return part * lags
    here, index = part
    side = meta[GRP] if here else 1 - meta[GRP]
    return pl.multiple_of((side * (count // 2) + index) * lags, 16)


def stage_kernel(starts, meta, paired, series, other, out, sems):
    days = series.shape[0]
    places = (pl.ds(0, HALO), pl.ds(HALO + days, HALO))
    middle = pltpu.make_async_copy(series, out.at[pl.ds(HALO, days), :], sems.at[0])
    middle.start()
    waits = [middle]
    for i, (ref, start) in enumerate(zip((paired, other), starts)):
        for even in (0, 1):
            copy = pltpu.make_async_copy(
                ref.at[pl.ds(start, HALO), :], out.at[places[even ^ i], :], sems.at[i + 1]
            )

            @pl.when(meta[EVEN] == even)
            def _():
                copy.start()

        waits.append(copy)
    for copy in waits:
        copy.wait()


def project_kernel(plan, parts, first_slot, count, modes, n_refs, finish, *refs):
    meta, source = refs[:2]
    pieces = refs[2 : 2 + n_refs]
    at = 2 + n_refs
    acc_in = None
    if first_slot > 0:
        acc_in = refs[at]
        at += 2
    out, bank, acc, scratch, sems = refs[at:]
    lags = WIDE // modes
    for copy in load_pieces(plan, pieces, bank, sems, meta):
        copy.wait()
    rows = acc.shape[0]
    for slot, part in enumerate(parts, first_slot):
        term = lax.dot_general(
            source[pl.ds(first_lag(meta, part, count, lags), rows), :],
            bank[slot * WIDE : (slot + 1) * WIDE, :],
            (((1,), (1,)), ((), ())),
            preferred_element_type=jnp.float32,
        )
        if slot > first_slot:
            acc[...] += term
        elif first_slot > 0:
            acc[...] = acc_in[...] + term
        else:
            acc[...] = term
    if finish:
        out[...] = pack_skewed(acc, scratch, rows - lags, modes)
    else:
        out[...] = acc[...]


def rebuild_kernel(parts, count, modes, n_sums, n_old, has_in, last, order, total_days, width, days, *refs):
    meta = refs[0]
    n_blocks = len(n_sums)
    at = 1
    sums = []
    for size in n_sums:
        sums.append(refs[at : at + size])
        at += size
    banks = refs[at : at + n_blocks]
    at += n_blocks
    olds = refs[at : at + n_old]
    at += n_old
    rec_in = None
    if has_in:
        rec_in = refs[at]
        at += 1
    rec_out = refs[at]
    at += 1
    if last:
        pcs_out = refs[at]
        at += 1
        stacked, scratch, done, pcs_done, sems = refs[at:]
    else:
        packed_out = refs[at : at + n_blocks]
        at += n_blocks
        stacked, scratch = refs[at:]
    lags = WIDE // modes
    groups = LANES // modes
    per_block = len(parts) // n_blocks
    cells = banks[0].shape[1]
    values = []
    for block in range(n_blocks):
        level = [ref[...] for ref in sums[block]]
        if len(level) == 1:
            level = [level[0][i] for i in range(level[0].shape[0])]
        while len(level) > 1:
            level = [level[i] + level[i + 1] for i in range(0, len(level), 2)]
        packed = level[0]
        day = groups * lax.broadcasted_iota(jnp.int32, packed.shape, 0)
        day = day + (groups - 1 - lane_group(packed.shape, modes)) + meta[DAY] - HALO
        packed = jnp.where((day >= 0) & (day <= total_days - width), packed, 0.0)
        values.append(packed)
        if not last:
            packed_out[block][...] = packed
        narrow = packed.astype(jnp.bfloat16).astype(jnp.float32)
        spread_skewed(narrow, scratch, modes)
        for index in range(per_block):
            slot = block * per_block + index
            lag = first_lag(meta, parts[slot], count, lags)
            low = pl.multiple_of(HALO - lag, 8)
            high = pl.multiple_of(HALO - groups - lag, 8)
            start = slot * WIDE
            stacked[:, start : start + LANES] = scratch[pl.ds(low, days), :].astype(jnp.bfloat16)
            stacked[:, start + LANES : start + WIDE] = scratch[pl.ds(high, days), :].astype(jnp.bfloat16)
    if last:
        day = meta[DAY] + lax.broadcasted_iota(jnp.int32, (days, 1), 0)
        windows = jnp.minimum(day, total_days - width) - jnp.maximum(0, day - width + 1) + 1
        scale = 1.0 / windows.astype(jnp.float32)
    copies = []
    depth = per_block * WIDE
    edges = list(range(0, cells, TILE)) + [cells]
    if last:
        edges.insert(-1, cells - TILE // 2)
        values = [ref[...] for ref in olds] + values
    for start, end in zip(edges, edges[1:]):
        tile = slice(start, end)
        if last and end == cells:
            unpack_modes([(meta[BLOCKS + i], v) for i, v in zip(order, values)], pcs_done, scratch, modes, HALO)
            copies.append(pltpu.make_async_copy(pcs_done, pcs_out, sems.at[len(copies)]))
            copies[-1].start()
        total = rec_in[:, tile] if has_in else None
        for block, bank in enumerate(banks):
            term = jnp.dot(
                stacked[:, block * depth : (block + 1) * depth],
                bank[:, tile],
                preferred_element_type=jnp.float32,
            )
            total = term if total is None else total + term
        if last:
            done[:, tile] = total * scale
            copies.append(pltpu.make_async_copy(done.at[:, tile], rec_out.at[:, tile], sems.at[len(copies)]))
            copies[-1].start()
        else:
            rec_out[:, tile] = total
    if last:
        for copy in copies:
            copy.wait()


def space(kind):
    return pl.BlockSpec(memory_space=kind)


def pinned(x):
    return pltpu.with_memory_space_constraint(x, pltpu.VMEM)


def left(x):
    return pltpu.with_memory_space_constraint(x, pltpu.HBM)


def flatten(pieces, row):
    arrays, plan = [], []
    for rows, choices in pieces:
        sources = []
        for array, start in choices:
            same = [i for i, other in enumerate(arrays) if other is array]
            if not same:
                arrays.append(array)
            sources.append((same[0] if same else len(arrays) - 1, start))
        plan.append((row, rows, sources))
        row += rows
    return plan, arrays


def stage(meta, paired, series, other, starts=(0, 0)):
    days, cells = series.shape
    return pl.pallas_call(
        functools.partial(stage_kernel, starts),
        out_shape=pltpu.VMEM((days + 2 * HALO, cells), jnp.bfloat16),
        in_specs=[space(pltpu.SMEM)] + [space(pltpu.HBM)] * 3,
        out_specs=space(pltpu.VMEM),
        scratch_shapes=[pltpu.SemaphoreType.DMA((3,))],
        compiler_params=pltpu.CompilerParams(vmem_limit_bytes=VMEM_BYTES),
        name="stage",
    )(meta, paired, series, other)


def cut_kernel(pieces, extended, half, meta, bank, series, *refs):
    outs, sems = refs[:-1], refs[-1]
    days = series.shape[0]
    copies = []
    for i, out in enumerate(outs):
        edge = i - extended if extended <= i < extended + 2 else None
        start, size = pieces[i if i <= extended else i - 1]
        first = pl.multiple_of(meta[GRP] * half + start, 16)
        copies.append(
            pltpu.make_async_copy(bank.at[pl.ds(first, size), :], out.at[pl.ds(0, size), :], sems.at[i])
        )
        copies[-1].start()
        if edge is not None:
            tail = meta[EVEN] if edge == 0 else (meta[DAY] == days).astype(jnp.int32)
            first = pl.multiple_of(tail * (days - HALO), 16)
            copies.append(
                pltpu.make_async_copy(
                    series.at[pl.ds(first, HALO), :], out.at[pl.ds(size, HALO), :], sems.at[len(outs) + edge]
                )
            )
            copies[-1].start()
    for copy in copies:
        copy.wait()


def cut(meta, bank, series, pieces, extended, half):
    cells = bank.shape[1]
    rows = [size for _, size in pieces]
    rows = rows[:extended] + [rows[extended] + HALO] * 2 + rows[extended + 1 :]
    return pl.pallas_call(
        functools.partial(cut_kernel, pieces, extended, half),
        out_shape=[jax.ShapeDtypeStruct((size, cells), bank.dtype) for size in rows],
        in_specs=[space(pltpu.SMEM)] + [space(pltpu.HBM)] * 2,
        out_specs=[space(pltpu.HBM)] * len(rows),
        scratch_shapes=[pltpu.SemaphoreType.DMA((len(rows) + 2,))],
        compiler_params=pltpu.CompilerParams(vmem_limit_bytes=VMEM_BYTES),
        name="cut",
    )(meta, left(bank), left(series))


def trim_kernel(*refs):
    sems = refs[-1]
    count = len(refs) // 2
    copies = []
    for i in range(count):
        out = refs[count + i]
        copies.append(pltpu.make_async_copy(refs[i].at[pl.ds(0, out.shape[0]), :], out, sems.at[i]))
        copies[-1].start()
    for copy in copies:
        copy.wait()


def trim(arrays, rows):
    return pl.pallas_call(
        trim_kernel,
        out_shape=[jax.ShapeDtypeStruct((rows, x.shape[1]), x.dtype) for x in arrays],
        in_specs=[space(pltpu.HBM)] * len(arrays),
        out_specs=[space(pltpu.HBM)] * len(arrays),
        scratch_shapes=[pltpu.SemaphoreType.DMA((len(arrays),))],
        compiler_params=pltpu.CompilerParams(vmem_limit_bytes=VMEM_BYTES),
        name="trim",
    )(*arrays)


def project(meta, source, pieces, parts, modes, width, before=None, finish=True):
    cells = source.shape[1]
    lags = WIDE // modes
    slots = width // lags
    first_slot = slots - len(parts) if before else 0
    plan, arrays = flatten(pieces, first_slot * WIDE)
    long = source.shape[0] - HALO
    rows = long + lags
    if finish:
        out = jax.ShapeDtypeStruct((long * modes // LANES, LANES), jnp.float32)
    else:
        out = pltpu.VMEM((rows, WIDE), jnp.float32)
    before = [pinned(x) for x in before] if before else []
    return pl.pallas_call(
        functools.partial(project_kernel, plan, parts, first_slot, slots, modes, len(arrays), finish),
        out_shape=(out, pltpu.VMEM((slots * WIDE, cells), jnp.bfloat16)),
        in_specs=[space(pltpu.SMEM), space(pltpu.VMEM)]
        + [space(pltpu.HBM)] * len(arrays)
        + [space(pltpu.VMEM)] * len(before),
        out_specs=(space(pltpu.VMEM), space(pltpu.VMEM)),
        scratch_shapes=[
            pltpu.VMEM((rows, WIDE), jnp.float32),
            pltpu.VMEM((rows - lags // 2, LANES), jnp.float32),
            pltpu.SemaphoreType.DMA((len(plan),)),
        ],
        input_output_aliases={3 + len(arrays): 1} if before else {},
        compiler_params=pltpu.CompilerParams(vmem_limit_bytes=VMEM_BYTES),
        cost_estimate=pl.CostEstimate(
            flops=2 * rows * len(parts) * WIDE * cells,
            bytes_accessed=2 * cells * len(parts) * WIDE,
            transcendentals=0,
        ),
        name="project",
    )(meta, pinned(source), *arrays, *before)


def rebuild(meta, blocks, modes, width, days, total_days, all_modes, so_far=None, old=(), last=False):
    lags = WIDE // modes
    banks = [pinned(block[2]) for block in blocks]
    parts = [part for block in blocks for part in block[3]]
    sums = [value for block in blocks for value in block[1]]
    cells = banks[0].shape[1]
    packed = sums[0].shape[-2:]
    has_in = so_far is not None
    olds = [value for _, value in old] if last else []
    order = tuple([index for index, _ in old] + [block[0] for block in blocks]) if last else ()
    scratch = [
        pltpu.VMEM((days, len(parts) * WIDE), jnp.bfloat16),
        pltpu.VMEM((days + HALO, LANES), jnp.float32),
    ]
    if last:
        out_shape = [jax.ShapeDtypeStruct((days, cells), jnp.float32)]
        out_shape += [jax.ShapeDtypeStruct((all_modes, days), jnp.float32)]
        out_specs = [space(pltpu.HBM), space(pltpu.HBM)]
        scratch += [
            pltpu.VMEM((days, cells), jnp.float32),
            pltpu.VMEM((all_modes, days), jnp.float32),
            pltpu.SemaphoreType.DMA((cells // TILE + 2,)),
        ]
    else:
        out_shape = [pltpu.VMEM((days, cells), jnp.float32)]
        out_shape += [jax.ShapeDtypeStruct(packed, jnp.float32) for _ in blocks]
        out_specs = [space(pltpu.VMEM)] * len(out_shape)
    before = 1 + len(sums) + len(banks)
    return pl.pallas_call(
        functools.partial(
            rebuild_kernel,
            parts,
            width // lags,
            modes,
            [len(block[1]) for block in blocks],
            len(olds),
            has_in,
            last,
            order,
            total_days,
            width,
            days,
        ),
        out_shape=out_shape,
        in_specs=[space(pltpu.SMEM)] + [space(pltpu.VMEM)] * (len(sums) + len(banks) + len(olds) + has_in),
        out_specs=out_specs,
        scratch_shapes=scratch,
        input_output_aliases={before: 0} if has_in and not last else {},
        compiler_params=pltpu.CompilerParams(vmem_limit_bytes=VMEM_BYTES),
        cost_estimate=pl.CostEstimate(
            flops=2 * days * len(parts) * WIDE * cells,
            bytes_accessed=4 * days * cells,
            transcendentals=0,
        ),
        name="rebuild",
    )(meta, *sums, *banks, *olds, *([pinned(so_far)] if has_in else []))


def exchange(packed):
    size = lax.axis_size("cell")
    return [packed] + [
        lax.ppermute(packed, "cell", [(i, i ^ step) for i in range(size)]) for step in range(1, size)
    ]


def on_device(series, eofs):
    width, modes, cells = eofs.shape
    days = series.shape[0]
    n = lax.axis_size("day")
    total_days = days * n
    day = lax.axis_index("day").astype(jnp.int32)
    grp = lax.axis_index("grp").astype(jnp.int32)
    n_parts = width * modes // WIDE
    bank = eofs.reshape(width * modes, cells)

    middle = ((day > 0) & (day < n - 1)).astype(jnp.int32)
    whole = list(range(n_parts))
    shape = dict(modes=modes, width=width)
    rest = dict(days=days, total_days=total_days, all_modes=modes * n)

    if n != 4 or lax.axis_size("grp") != 2 or n_parts != 4:
        every = lax.all_gather(bank, "day", axis=0, tiled=False)
        meta = jnp.stack([day * days, grp, middle, 1 - day % 2] + [jnp.int32(i) for i in range(n)])
        behind = lax.ppermute(series[days - HALO :], "day", [(i, i + 1) for i in range(n - 1)])
        ahead = lax.ppermute(series[:HALO], "day", [(i + 1, i) for i in range(n - 1)])
        even = day % 2 == 0
        source = stage(meta, jnp.where(even, ahead, behind), series, jnp.where(even, behind, ahead))
        rec, old = None, []
        for block in range(n):
            pieces = [(width * modes, [(every[block], 0)])]
            packed, bank = project(meta, source, pieces, whole, **shape)
            rec, small = rebuild(
                meta, [(block, exchange(packed), bank, whole)], so_far=rec, old=old, last=block == n - 1, **shape, **rest
            )
            old.append((block, small))
        return small.T, rec

    entry = lax.broadcasted_iota(jnp.int32, (8,), 0)
    meta = jnp.zeros((8,), jnp.int32)
    low = day // 2
    for i, value in enumerate([day * days, grp, middle, 1 - day % 2, day, day + 1 - 2 * (day % 2), 2 - low, 3 - 3 * low]):
        meta = jnp.where(entry == i, value, meta)
    half = width * modes // 2
    cuts = CUTS
    pieces, row = [], 0
    for size in cuts:
        pieces.append((row * half // sum(cuts), size * half // sum(cuts)))
        row += size
    held = {}
    parts_out = cut(meta, bank, series, pieces, EXTENDED, half)
    for i in range(len(pieces)):
        held["own", i] = parts_out[i if i <= EXTENDED else i + 1]
    extended = {"p1": parts_out[EXTENDED], "p2": parts_out[EXTENDED + 1]}
    n_pieces = len(pieces)
    last_piece = n_pieces - 1
    sent_from = {
        "p1": "own", "p2": "own", "q1": "p2", "q2": "p1", "f": "q2",
        "yp1": "p1", "yp2": "p2", "yq1": "q1", "yq2": "q2", "yf": "f", "h": "yp1", "g": "h",
    }

    def across(array, members):
        return lax.ppermute(
            array,
            ("grp", "day"),
            [(g * n + d, (1 - g) * n + d) for g in (0, 1) for d in members],
        )

    def send(name, array):
        if name == "p1":
            return lax.ppermute(array, "day", PAIRED)
        if name in ("p2", "q2", "h"):
            return lax.ppermute(array, "day", MIDDLE)
        if name in ("q1", "f", "g"):
            return lax.ppermute(array, "day", OUTWARD)
        return across(array, {"yp1": ENDS + MIDS, "yp2": MIDS, "yq1": ENDS, "yq2": MIDS, "yf": ENDS}[name])

    halves = [(True, 0), (True, 1), (False, 0), (False, 1)]
    arrivals = {"a": ("p1",), "b": ("q1", "p2"), "c": ("f", "q2")}
    place = {"own": 0, "a": 1, "b": 2, "c": 3}

    def pieces_of(block, which=range(4)):
        if block == "own":
            return [(width * modes, [(bank, 0)])]
        names = arrivals[block]
        picked = []
        for side in ("", "y"):
            for i, (start, size) in enumerate(pieces):
                ours = [side + name for name in names]
                if block == "c" and side == "y":
                    ours = ["g" if i == last_piece else "yf", "h"]
                choices = [held[name, i] for name in ours]
                for chunk in range(half // WIDE):
                    first = max(start, chunk * WIDE)
                    end = min(start + size, (chunk + 1) * WIDE)
                    if first < end and (side == "y") * (half // WIDE) + chunk in which:
                        picked.append((end - first, [(array, first - start) for array in choices]))
        return picked

    def run(kind, which):
        if kind == "after":
            key, other = which
            held[key], held[other] = lax.optimization_barrier((held[key], held[other]))
        elif kind == "stage":
            starts = (pieces[EXTENDED][1],) * 2
            held["source"] = stage(meta, held["long", "p1"], series, held["long", "p2"], starts)
        elif kind == "project":
            source = held["source"]
            if which == "c1":
                held["acc"], held["bank", "c"] = project(
                    meta, source, pieces_of("c", (0, 1, 2)), halves[:3], finish=False, **shape
                )
            elif which == "c2":
                before = (held["acc"], held["bank", "c"])
                held["packed", "c"], held["bank", "c"] = project(
                    meta, source, pieces_of("c", (3,)), halves[3:], before=before, **shape
                )
            else:
                parts = whole if which == "own" else halves
                held["packed", which], held["bank", which] = project(
                    meta, source, pieces_of(which), parts, **shape
                )
        elif kind == "exchange":
            if which == "c":
                held["sum", which] = exchange(held["packed", which])
            else:
                held["sum", which] = [lax.all_gather(held["packed", which], "cell", axis=0)]
        else:
            blocks = []
            for block in which:
                sums = held["sum", block]
                parts = whole if block == "own" else halves
                blocks.append((place[block], sums, held["bank", block], parts))
            last = "c" in which
            old = [(place[b], held["old", b]) for b in place if ("old", b) in held]
            done = rebuild(meta, blocks, so_far=held.get("rec"), old=old, last=last, **shape, **rest)
            held["rec"] = done[0]
            if last:
                held["pcs"] = done[1]
            else:
                held.update({("old", block): value for block, value in zip(which, done[1:])})

    tasks = {
        3: [("stage", None), ("project", "own")],
        4: [("exchange", "own")],
        5: [("rebuild", ("own",))],
        7: [("project", "a")],
        8: [("exchange", "a")],
        13: [
            ("project", "b"),
            ("after", (("bank", "a"), ("packed", "b"))),
            ("exchange", "b"),
            ("project", "c1"),
            ("rebuild", ("a",)),
        ],
        14: [("project", "c2")],
        15: [("exchange", "c"), ("rebuild", ("b",))],
        16: [("rebuild", ("c",))],
    }
    lag = 2
    along = [[("p1", i), ("p2", i)] for i in range(n_pieces)]
    along += [[("q2", i), ("q1", i)] for i in range(n_pieces)]
    along += [[("f", i), ("h", (i - 1) % n_pieces)] for i in range(n_pieces)]
    swaps = [[("yp1", i)] for i in range(n_pieces)]
    swaps += [[("yp2", i), ("yq1", i)] for i in range(n_pieces)]
    swaps += [[("yf", i)] for i in range(last_piece)]
    along.append([("g", last_piece)])
    last_slot = len(along) - 1

    done_at = []
    for slot in range(last_slot + 6):
        sends = list(along[slot]) if slot <= last_slot else []
        if 0 <= slot - lag < len(swaps):
            sends = swaps[slot - lag] + sends
        if lag <= slot <= last_slot:
            keys = [(sent_from[name], i) for name, i in sends] + done_at[slot - lag]
            for kind, which in tasks.get(slot, []):
                if kind == "exchange":
                    keys.append(("packed", which))
                if kind == "rebuild":
                    keys += [("bank", block) for block in which]
            keys = [key for key in dict.fromkeys(keys) if key in held]
            values = lax.optimization_barrier(tuple(held[key] for key in keys))
            held.update(zip(keys, values))
        before = dict(held)
        if slot == EXTENDED + lag:
            long = [held["long", name] for name in ("p1", "p2")]
            held["p1", EXTENDED], held["p2", EXTENDED] = trim(long, pieces[EXTENDED][1])
        for name, i in sends:
            if i == EXTENDED and name in extended:
                held["long", name] = send(name, extended[name])
                continue
            held[name, i] = send(name, held[sent_from[name], i])
        for task in tasks.get(slot, []):
            run(*task)
        done_at.append([key for key, value in held.items() if before.get(key) is not value])
    return held["pcs"].T, held["rec"]


def solution(mesh):
    return jax.shard_map(
        on_device,
        mesh=mesh,
        in_specs=(P(("grp", "day"), "cell"), P(None, "day", "cell")),
        out_specs=(P(("grp", "day"), None), P(("grp", "day"), "cell")),
        check_vma=False,
    )
```
